256 devices in a mesh: gx: 32 (over x, y, core), gy: 8 (over z).
Axes of the slice: x: 4, y: 4, z: 8, core: 2. Of those that a mesh axis runs over, the one named last changes fastest.
Arguments:
- pressure: float32 [512, 512, 512], P('gx', 'gy'), may hold values from -3 to 3
- permeability: float32 [512, 512, 512], P('gx', 'gy'), may hold values from 0.1 to 1
- kernel: float32 [2, 12288, 12288], P(None, 'gx', 'gy'), may hold values from -0.4330127 to 0.4330127
- slip_rate: float32 [12288], P(('gx', 'gy')), may hold values from 0.1 to 1
- aging_state: float32 [12288], P(('gx', 'gy')), may hold values from 0.5 to 5
- normal_stress: float32 [12288], P(('gx', 'gy')), may hold values from 50 to 80
- shear_stress: float32 [12288], P(('gx', 'gy')), may hold values from 33 to 45
- direct_effect: float32 [12288], P(('gx', 'gy')), may hold values from 0.01 to 0.02
- evolution_effect: float32 [12288], P(('gx', 'gy')), may hold values from 0.01 to 0.03
- slip_distance: float32 [12288], P(('gx', 'gy')), may hold values from 0.2 to 1
- tri_owner: int32 [12288, 1], P(('gx', 'gy')), may hold values from 0 to 31; in each aligned block of 48 rows (0 to 47, 48 to 95, ...) at most 3 rows name the same one
- tri_cell: int32 [12288], P(('gx', 'gy')), may hold values from 0 to 524287
Outputs:
- pressure_next: float32 [512, 512, 512], P('gx', 'gy')
- state_next: float32 [12288], P(('gx', 'gy'))
- log_rate: float32 [12288], P(('gx', 'gy'))
The draws below stay inside these ranges and needn't reach their ends.
Inputs may be any that keep to these rules, and one draw needn't show every extreme that they name: `tri_owner`: at most 3 of the 48 triangles of one device name one owner, and in every draw some owner is named by exactly 3 triangles of some device.
All inputs are finite; a program needn't handle non-finite values.
Results may differ from the reference program's by a relative error of at most 0.000092.
Values sent between devices are 32-bit elements; how exact they have to be, the bound alone decides.
No kernel may reach another device: no remote copies, remote signals or barrier semaphores. Data moves between devices by JAX's collectives and lax.ppermute only.
A program may use at most 64 MiB of HBM per device.

```python
import math
import jax
import jax.numpy as jnp
import numpy as np
from jax import lax

CX = 16
CY = 64
NZ = 512
SWEEPS = 3
TRI_DEV = 48
NTRI = 12288
CAP = 3
NX = 512
NY = 512
N_GX = 32
N_GY = 8


def set_ends(values, key, least, top_value):
    spot = [jax.random.randint(jax.random.fold_in(key, axis), (), 0, length) for axis, length in enumerate(values.shape)]
    main_axis = values.shape.index(max(values.shape))
    beside = spot[:main_axis] + [(spot[main_axis] + 1) % values.shape[main_axis]] + spot[main_axis + 1:]
    return values.at[tuple(spot)].set(least).at[tuple(beside)].set(top_value)


def level_of(rng, dims, pieces, smallest, top_value):
    def one(position, shards_of):
        heights = jax.random.uniform(jax.random.fold_in(jax.random.fold_in(rng, 6), position), (shards_of,), jnp.float32, smallest / len(pieces), top_value / len(pieces))
        return jnp.repeat(jnp.exp(heights), dims[position] // shards_of).reshape((-1,) + (1,) * (len(dims) - position - 1))

    level = one(*pieces[0])
    for cut in pieces[1:]:
        level = level * one(*cut)
    return level


def routed_block(rng, own, number, rows, amount, top, limit, skew):
    sequence = jax.random.permutation(rng, amount)
    packed, common = shares(amount, rows * top, limit, skew, True), shares(amount, rows * top, limit, skew, False)
    places = jnp.arange(amount)

    def named(lengths, offset_by):
        used = int((lengths > 0).sum())
        fixed = max(1, used // 4)
        passed = fixed + (places - fixed + offset_by * (used - fixed)) % max(1, amount - fixed)
        return jnp.zeros((amount,), jnp.int32).at[sequence[jnp.where(places < fixed, places, passed)]].set(jnp.asarray(lengths, jnp.int32))

    lengths = jnp.where(number % 4 == 0, named(packed, number // 4), named(common, number - number // 4 - 1))
    mixed = jax.random.permutation(jax.random.fold_in(own, 3), amount)
    source_of, receiver = mixed[0:amount // 2 * 2:2], mixed[1:amount // 2 * 2:2]
    slack = jnp.minimum(lengths[source_of] - 1, limit - lengths[receiver]) // 2
    slack = jnp.where((source_of == sequence[0]) | (receiver == sequence[0]) | (lengths[receiver] == 0), 0, jnp.maximum(slack, 0))
    passed = jax.random.randint(jax.random.fold_in(own, 4), (amount // 2,), 0, 1 << 20) % (slack + 1)
    lengths = lengths.at[source_of].add(-passed).at[receiver].add(passed)
    labels = jnp.searchsorted(jnp.cumsum(lengths), jnp.arange(rows * top), side="right").astype(jnp.int32)
    table = labels.reshape(top, rows).T
    table = table[jax.random.permutation(jax.random.fold_in(own, 1), rows)]
    offset_by = jax.random.randint(jax.random.fold_in(own, 2), (rows, 1), 0, top)
    return jnp.take_along_axis(table, (jnp.arange(top)[None, :] + offset_by) % top, axis=1)


def shares(count, total, bound, skew, full):
    loads = [(1 << 20) // math.isqrt(grade ** skew) + 1 for grade in range(1, count + 1)]
    largest = bound if full else min(bound, max(-(-total // count), total * loads[0] // sum(loads)))
    least = 1 if total - largest >= count - 1 else 0
    counts, spare = [largest] + [least] * (count - 1), total - largest - least * (count - 1)
    while spare > 0:
        candidates = [i for i in range(1, count) if counts[i] < largest] or [i for i in range(1, count) if counts[i] < bound]
        whole, left = sum([loads[i] for i in candidates]), spare
        for i in candidates:
            more = min(bound - counts[i], max(1, left * loads[i] // whole), spare)
            counts[i] = counts[i] + more
            spare = spare - more
    return np.array(counts)


def scatter_about(rng, shape, spread, most, pieces=(), held_as=jnp.bfloat16):
    array = spread * jax.random.normal(rng, shape, jnp.float32)
    if pieces:
        array = array * level_of(rng, shape, pieces, -0.22, 0.18)
    return jnp.clip(array, -most, most).astype(held_as)


def setup_inputs(seed: int = 0) -> dict:
    splits = jax.random.split(jax.random.key(seed), 13)
    pressure = scatter_about(splits[0], (NX, NY, NZ), 1.0, 3.0, ((0, 32), (1, 8)), jnp.float32)
    permeability = jnp.clip(jnp.exp(math.log(1.0) - 2.3025851 * jax.random.uniform(splits[1], (NX, NY, NZ), jnp.float32) ** level_of(splits[1], (NX, NY, NZ), ((0, 32), (1, 8)), -0.2, 0.2)), 0.1, 1.0)
    kernel = scatter_about(splits[2], (2, NTRI, NTRI), (8.0 / NTRI ** 0.5), 0.4330127, ((1, 32), (2, 8)), jnp.float32)
    slip_rate = jnp.clip(jnp.exp(math.log(1.0) - 2.3025851 * jax.random.uniform(splits[3], (NTRI,), jnp.float32) ** level_of(splits[3], (NTRI,), ((0, 256),), -0.2, 0.2)), 0.1, 1.0)
    aging_state = jnp.clip(jnp.exp(math.log(5.0) - 2.3025851 * jax.random.uniform(splits[4], (NTRI,), jnp.float32) ** level_of(splits[4], (NTRI,), ((0, 256),), -0.2, 0.2)), 0.5, 5.0)
    normal_stress = jnp.clip(50.0 + 30.0 * jax.random.uniform(splits[5], (NTRI,), jnp.float32) ** level_of(splits[5], (NTRI,), ((0, 256),), -0.2, 0.2), 50.0, 80.0)
    shear_stress = jnp.clip(33.0 + 12.0 * jax.random.uniform(splits[6], (NTRI,), jnp.float32) ** level_of(splits[6], (NTRI,), ((0, 256),), -0.2, 0.2), 33.0, 45.0)
    direct_effect = jnp.clip(jnp.exp(math.log(0.02) - 0.6931472 * jax.random.uniform(splits[7], (NTRI,), jnp.float32) ** level_of(splits[7], (NTRI,), ((0, 256),), -0.2, 0.2)), 0.01, 0.02)
    evolution_effect = jnp.clip(jnp.exp(math.log(0.03) - 1.0986123 * jax.random.uniform(splits[8], (NTRI,), jnp.float32) ** level_of(splits[8], (NTRI,), ((0, 256),), -0.2, 0.2)), 0.01, 0.03)
    slip_distance = jnp.clip(jnp.exp(math.log(1.0) - 1.609438 * jax.random.uniform(splits[9], (NTRI,), jnp.float32) ** level_of(splits[9], (NTRI,), ((0, 256),), -0.2, 0.2)), 0.2, 1.0)
    tri_owner_keys = jax.random.split(jax.random.fold_in(splits[10], 1), NTRI // TRI_DEV)
    tri_owner_turns = jax.random.permutation(jax.random.fold_in(splits[10], 3), NTRI // TRI_DEV)
    tri_owner = jax.vmap(lambda own, number: routed_block(jax.random.fold_in(splits[10], 2), own, number, TRI_DEV, N_GX, 1, CAP, 2))(tri_owner_keys, tri_owner_turns).reshape((NTRI, 1))
    tri_cell = set_ends(jax.random.randint(splits[11], (NTRI,), 0, CX * CY * NZ), jax.random.fold_in(splits[11], 1), 0, (CX * CY * NZ) - 1).astype(jnp.int32)
    return {"pressure": pressure, "permeability": permeability, "kernel": kernel, "slip_rate": slip_rate, "aging_state": aging_state, "normal_stress": normal_stress, "shear_stress": shear_stress, "direct_effect": direct_effect, "evolution_effect": evolution_effect, "slip_distance": slip_distance, "tri_owner": tri_owner, "tri_cell": tri_cell}


conductance = 0.15
step_time = 1.0
heal_time = 0.5
friction_ref = 0.6
neighbours = ((1, 0, 0), (-1, 0, 0), (0, 1, 0), (0, -1, 0), (0, 0, 1), (0, 0, -1))

def shifted(values, step_x, step_y, step_z):
    return values[1 + step_x:values.shape[0] - 1 + step_x, 1 + step_y:values.shape[1] - 1 + step_y, 1 + step_z:values.shape[2] - 1 + step_z]

def explicit_step(padded_p, padded_k):
    full_p = jnp.pad(padded_p, ((0, 0), (0, 0), (1, 1)))
    full_k = jnp.pad(padded_k, ((0, 0), (0, 0), (1, 1)))
    centre_p = shifted(full_p, 0, 0, 0)
    centre_k = shifted(full_k, 0, 0, 0)
    flux = jnp.zeros_like(centre_p)
    for offset in neighbours:
        other_p = shifted(full_p, offset[0], offset[1], offset[2])
        other_k = shifted(full_k, offset[0], offset[1], offset[2])
        flux = flux + jnp.sqrt(centre_k * other_k) * (other_p - centre_p)
    return centre_p + conductance * flux

def reference(pressure, permeability, kernel, slip_rate, aging_state, normal_stress, shear_stress, direct_effect, evolution_effect, slip_distance, tri_owner, tri_cell):
    padded_k = jnp.pad(permeability, ((1, 1), (1, 1), (0, 0)))
    pressure_field = pressure
    for repeat in range(SWEEPS):
        pressure_field = explicit_step(jnp.pad(pressure_field, ((1, 1), (1, 1), (0, 0))), padded_k)
    triangles = jnp.arange(NTRI, dtype=jnp.int32)
    column_dev = triangles // TRI_DEV % N_GY
    owners = tri_owner[:, 0].astype(jnp.int32)
    pos_x = owners * CX + tri_cell // (CY * NZ)
    pos_y = column_dev * CY + tri_cell // NZ % CY
    pos_z = tri_cell % NZ
    fault_pressure = pressure_field[pos_x, pos_y, pos_z]
    rates = jnp.dot(kernel.reshape(2 * NTRI, NTRI), slip_rate, precision=lax.Precision.HIGHEST).reshape(2, NTRI)
    shear = shear_stress + step_time * rates[0]
    effective = normal_stress + step_time * rates[1] - fault_pressure
    ratio = slip_distance / slip_rate
    state_next = ratio + (aging_state - ratio) * jnp.exp(-heal_time / ratio)
    log_rate = (shear / effective - friction_ref - evolution_effect * jnp.log(state_next / slip_distance)) / direct_effect
    return (pressure_field, state_next, log_rate)
```

```python
import jax
import jax.numpy as jnp
from jax import lax
from jax.experimental import pallas as pl
from jax.experimental.pallas import tpu as pltpu
from jax.sharding import PartitionSpec as P

NGX, NGY = 32, 8
CX, CY, NZ, TRI = 16, 64, 512, 48
HALO = 3
ROWS = 80
LANES = 128
CHUNKS = NZ // LANES
conductance = 0.15
step_time = 1.0
heal_time = 0.5
friction_ref = 0.6
F32 = jnp.float32
VMEM = pltpu.VMEM
ANY = pl.ANY

X_MOVE = (2, 1, 2, 1, 0, 3, 0, 3)
Y_MOVE = (1, 1, 0, 0, 0, 0, 1, 1)
X_CODE = sum(v << (2 * i) for i, v in enumerate(X_MOVE))
Y_CODE = sum(v << i for i, v in enumerate(Y_MOVE))


def landing(group, other):
    delta = (other - group) & 7
    x = ((group >> 1) + ((X_CODE >> (2 * delta)) & 3)) & 3
    y = (group & 1) ^ ((Y_CODE >> delta) & 1)
    return 2 * x + y


SLIP_MOVES = [
    ((4 * g + r) * NGY + j, (4 * landing(g, j) + r) * NGY + g) for g in range(8) for r in range(4) for j in range(NGY)
]
X_UP = [(i, i + 1) for i in range(NGX - 1)]
X_DOWN = [(j, i) for i, j in X_UP]
Y_UP = [(i, i + 1) for i in range(NGY - 1)]
Y_DOWN = [(j, i) for i, j in Y_UP]


def spec(space=VMEM):
    return pl.BlockSpec(memory_space=space)


def shape(*dims, dtype=F32):
    return jax.ShapeDtypeStruct(dims, dtype)


def pack_kernel(p, k, x_up, x_down, y_up, y_down, tiles, sems):
    copies = [
        pltpu.make_async_copy(src, dst, sems.at[n])
        for n, (src, dst) in enumerate(
            (
                (p.at[:, pl.ds(CY - 8, 8), :], tiles.at[0]),
                (k.at[:, pl.ds(CY - 8, 8), :], tiles.at[1]),
                (p.at[:, pl.ds(0, 8), :], tiles.at[2]),
                (k.at[:, pl.ds(0, 8), :], tiles.at[3]),
                (p.at[pl.ds(CX - HALO, HALO)], x_up.at[pl.ds(0, HALO)]),
                (k.at[pl.ds(CX - HALO, HALO)], x_up.at[pl.ds(HALO, HALO)]),
                (p.at[pl.ds(0, HALO)], x_down.at[pl.ds(0, HALO)]),
                (k.at[pl.ds(0, HALO)], x_down.at[pl.ds(HALO, HALO)]),
            )
        )
    ]
    for copy in copies:
        copy.start()
    for copy in copies[:4]:
        copy.wait()
    row = lax.broadcasted_iota(jnp.int32, (8, NZ), 0)

    def plane(x, carry):
        y_up[x] = jnp.where(row >= 5, tiles[0, x], pltpu.roll(tiles[1, x], 3, 0))
        y_down[x] = jnp.where(row < 3, tiles[2, x], pltpu.roll(tiles[3, x], 5, 0))
        return carry

    lax.fori_loop(0, CX, plane, 0)
    for copy in copies[4:]:
        copy.wait()


def pack(p, k):
    return pl.pallas_call(
        pack_kernel,
        out_shape=(
            shape(2 * HALO, CY, NZ),
            shape(2 * HALO, CY, NZ),
            shape(CX, 8, NZ),
            shape(CX, 8, NZ),
        ),
        in_specs=[spec(ANY)] * 2,
        out_specs=(spec(ANY), spec(ANY), spec(), spec()),
        scratch_shapes=[VMEM((4, CX, 8, NZ), F32), pltpu.SemaphoreType.DMA((8,))],
        compiler_params=pltpu.CompilerParams(vmem_limit_bytes=8 << 20),
        name="pack",
    )(p, k)


def rank_row(owner_row, owner_column):
    same = owner_column == owner_row
    first = lax.broadcasted_iota(jnp.int32, (TRI, TRI), 0)
    second = lax.broadcasted_iota(jnp.int32, (TRI, TRI), 1)
    hits = jnp.where(jnp.logical_and(same, first < second), 1.0, 0.0)
    return jnp.sum(hits, axis=0, keepdims=True)


def request_kernel(owner_row, owner_column, cell_row, out):
    owners = owner_row[...]
    rank = rank_row(owners, owner_column[...])
    cells = cell_row[...].astype(F32)
    lane = lax.broadcasted_iota(jnp.int32, (NGX, LANES), 1)
    named = lax.broadcasted_iota(jnp.int32, (NGX, TRI), 0) == owners
    value = jnp.zeros((NGX, LANES), F32)
    for c in range(3):
        asked = jnp.where(jnp.logical_and(named, rank == float(c)), cells, 0.0)
        value = jnp.where(lane == TRI + c, jnp.sum(asked, axis=1, keepdims=True), value)
    out[...] = value


def requests_of(owner_row, owner_column, cell_row):
    return pl.pallas_call(
        request_kernel,
        out_shape=shape(NGX, LANES),
        in_specs=[spec()] * 3,
        out_specs=spec(),
        name="requests",
    )(owner_row, owner_column, cell_row)


def rates_kernel(arrived, kernel, out, cells, acc):
    gy = lax.axis_index("gy")
    lane = lax.broadcasted_iota(jnp.int32, (1, LANES), 1)
    chunks = [jnp.zeros((1, LANES), F32) for _ in range(12)]
    for j in range(NGY):
        spot = landing(gy, j)
        for r in range(4):
            start = (r * NGY + j) * TRI
            chunk, offset = divmod(start, LANES)
            row = pltpu.roll(arrived[pl.ds(4 * spot + r, 1), :], offset, 1)
            inside = jnp.logical_and(lane >= offset, lane < offset + TRI)
            chunks[chunk] = jnp.where(inside, row, chunks[chunk])
            if offset + TRI > LANES:
                chunks[chunk + 1] = jnp.where(lane < offset + TRI - LANES, row, chunks[chunk + 1])
    cells[...] = pltpu.roll(arrived[...], LANES - TRI, 1).astype(jnp.int32)
    wide = [jnp.broadcast_to(c, (8, LANES)) for c in chunks]

    for part in range(2):

        def tile(t, carry):
            rows = pl.ds(pl.multiple_of(t * 8, 8), 8)
            terms = [kernel[part, rows, pl.ds(LANES * c, LANES)] * wide[c] for c in range(12)]
            while len(terms) > 1:
                terms = [a + b for a, b in zip(terms[::2], terms[1::2])] + terms[len(terms) // 2 * 2 :]
            dest = (t // 6) * 96 + part * TRI + (t % 6) * 8
            acc[pl.ds(pl.multiple_of(dest, 8), 8), :] = terms[0]
            return carry

        lax.fori_loop(0, 48, tile, 0, unroll=4)
    row8 = lax.broadcasted_iota(jnp.int32, (8, LANES), 0)
    total = jnp.zeros((8, 2 * TRI), F32)
    for j in range(NGY):
        total = total + lax.dot_general(
            jnp.where(row8 == j, 1.0, 0.0),
            acc[pl.ds(2 * TRI * j, 2 * TRI), :],
            (((1,), (1,)), ((), ())),
            precision=lax.Precision.HIGHEST,
            preferred_element_type=F32,
        )
    out[...] = jnp.zeros((8, LANES), F32)
    out[:, 0 : 2 * TRI] = total


def partial_rates(arrived, kernel):
    return pl.pallas_call(
        rates_kernel,
        out_shape=(shape(NGY, LANES), shape(NGX, LANES, dtype=jnp.int32)),
        in_specs=[spec()] * 2,
        out_specs=(spec(), spec()),
        scratch_shapes=[VMEM((768, LANES), F32)],
        compiler_params=pltpu.CompilerParams(vmem_limit_bytes=16 << 20),
        name="rates",
    )(arrived, kernel)


def around(ref, x, before, after, row, lane):
    rows = pl.ds(row, 8)
    centre = [ref[x * CHUNKS + i, rows, :] for i in range(CHUNKS)]
    left = [pltpu.roll(v, 1, 1) for v in centre]
    right = [pltpu.roll(v, LANES - 1, 1) for v in centre]
    sums = []
    for i in range(CHUNKS):
        below = left[i - 1] if i else 0.0
        above = right[i + 1] if i + 1 < CHUNKS else 0.0
        z = jnp.where(lane == 0, below, left[i]) + jnp.where(lane == LANES - 1, above, right[i])
        y = ref[x * CHUNKS + i, pl.ds(row - 1, 8), :] + ref[x * CHUNKS + i, pl.ds(row + 1, 8), :]
        xs = ref[before * CHUNKS + i, rows, :] + ref[after * CHUNKS + i, rows, :]
        sums.append((xs + y) + z)
    return centre, sums


def stretch(first, last):
    return range(first, last, 8)


def inner_kernel(p, k, y_up, y_down, out, s_edge, q_edge, a_edge, q1_edge, q2_edge, s, q, a, q1, q2, field, sem):
    lane = lax.broadcasted_iota(jnp.int32, (8, LANES), 1)
    row = lax.broadcasted_iota(jnp.int32, (8, LANES), 0)

    def convert(x, carry):
        for i in range(CHUNKS):
            lanes = pl.ds(LANES * i, LANES)
            low, high = y_up[x, :, lanes], y_down[x, :, lanes]
            root = jnp.sqrt(jnp.where(row >= 5, pltpu.roll(low, 5, 0), 0.0))
            s[x * CHUNKS + i, 0:8, :] = root
            q[x * CHUNKS + i, 0:8, :] = root * low
            root = jnp.sqrt(jnp.where(row < 3, pltpu.roll(high, 3, 0), 0.0))
            s[x * CHUNKS + i, 72:80, :] = root
            q[x * CHUNKS + i, 72:80, :] = root * high
            for t in range(CY // 8):
                root = jnp.sqrt(k[x, 8 * t : 8 * t + 8, lanes])
                s[x * CHUNKS + i, 8 * t + 8 : 8 * t + 16, :] = root
                q[x * CHUNKS + i, 8 * t + 8 : 8 * t + 16, :] = root * p[x, 8 * t : 8 * t + 8, lanes]
        return carry

    lax.fori_loop(0, CX, convert, 0)

    def first(x, carry):
        for r in stretch(6, 74):
            root, sums = around(s, x, x - 1, x + 1, r, lane)
            centre, total = around(q, x, x - 1, x + 1, r, lane)
            for i in range(CHUNKS):
                scaled = conductance * root[i]
                keep = 1.0 - scaled * sums[i]
                a[x * CHUNKS + i, pl.ds(r, 8), :] = keep
                q1[x * CHUNKS + i, pl.ds(r, 8), :] = keep * centre[i] + (scaled * root[i]) * total[i]
        return carry

    lax.fori_loop(1, CX - 1, first, 0)

    def second(x, carry):
        for r in stretch(7, 73):
            centre, total = around(q1, x, x - 1, x + 1, r, lane)
            for i in range(CHUNKS):
                root = s[x * CHUNKS + i, pl.ds(r, 8), :]
                keep = a[x * CHUNKS + i, pl.ds(r, 8), :]
                q2[x * CHUNKS + i, pl.ds(r, 8), :] = keep * centre[i] + (conductance * root * root) * total[i]
        return carry

    lax.fori_loop(2, CX - 2, second, 0)

    def third(x, carry):
        for r in stretch(8, 72):
            centre, total = around(q2, x, x - 1, x + 1, r, lane)
            for i in range(CHUNKS):
                root = s[x * CHUNKS + i, pl.ds(r, 8), :]
                keep = a[x * CHUNKS + i, pl.ds(r, 8), :]
                field[x - HALO, pl.ds(r - 8, 8), pl.ds(LANES * i, LANES)] = (
                    keep * centre[i] / root + (conductance * root) * total[i]
                )
        return carry

    lax.fori_loop(HALO, CX - HALO, third, 0)
    copy = pltpu.make_async_copy(field, out.at[pl.ds(HALO, CX - 2 * HALO)], sem)
    copy.start()
    for source, edge, depths in (
        (s, s_edge, (0, 1, 2)),
        (q, q_edge, (0, 1)),
        (a, a_edge, (1, 2)),
        (q1, q1_edge, (1, 2)),
        (q2, q2_edge, (2, 3)),
    ):
        for n, depth in enumerate(depths):
            for side, x in enumerate((depth, CX - 1 - depth)):
                edge[side, pl.ds(n * CHUNKS, CHUNKS)] = source[pl.ds(x * CHUNKS, CHUNKS)]
    copy.wait()


def block(planes):
    return VMEM((planes * CHUNKS, ROWS, LANES), F32)


def inner(p, k, y_up, y_down):
    return pl.pallas_call(
        inner_kernel,
        out_shape=(shape(CX, CY, NZ),) + tuple(shape(2, n * CHUNKS, ROWS, LANES) for n in (3, 2, 2, 2, 2)),
        in_specs=[spec()] * 4,
        out_specs=(spec(ANY),) + (spec(),) * 5,
        scratch_shapes=[block(CX) for _ in range(5)]
        + [VMEM((CX - 2 * HALO, CY, NZ), F32), pltpu.SemaphoreType.DMA(())],
        compiler_params=pltpu.CompilerParams(vmem_limit_bytes=40 << 20),
        cost_estimate=pl.CostEstimate(flops=40_000_000, bytes_accessed=12_000_000, transcendentals=0),
        name="inner",
    )(p, k, y_up, y_down)


def outer_kernel(
    field, s_edge, q_edge, a_edge, q1_edge, q2_edge, x_up, x_down, c_up, c_down, cells, out, answers, s, q, a, q1, q2, full, asked, sems
):
    del field
    ask = pltpu.make_async_copy(cells, asked, sems.at[0])
    ask.start()
    fill = pltpu.make_async_copy(
        out.at[pl.ds(HALO, CX - 2 * HALO)], full.at[pl.ds(HALO, CX - 2 * HALO)], sems.at[1]
    )
    fill.start()
    lane = lax.broadcasted_iota(jnp.int32, (8, LANES), 1)
    row = lax.broadcasted_iota(jnp.int32, (8, LANES), 0)
    zero = jnp.zeros((8, LANES), F32)
    stores = []
    for side, (wide, corner) in enumerate(((x_up, c_up), (x_down, c_down))):
        for target, edge, start in ((s, s_edge, 3), (q, q_edge, 3), (a, a_edge, 4), (q1, q1_edge, 4), (q2, q2_edge, 5)):
            count = edge.shape[1]
            target[pl.ds(start * CHUNKS, count)] = edge[side]
        for d in range(HALO):
            plane = d if side == 0 else HALO - 1 - d
            for i in range(CHUNKS):
                lanes = pl.ds(LANES * i, LANES)
                n = d * CHUNKS + i
                if d == 0:
                    for ref in (s, q):
                        ref[n, 0:8, :] = zero
                        ref[n, 72:80, :] = zero
                else:
                    c = d - 1 if side == 0 else 2 - d
                    low, high = corner[c, :, lanes], corner[2 + c, :, lanes]
                    root = jnp.sqrt(jnp.where(row >= 5, pltpu.roll(low, 5, 0), 0.0))
                    s[n, 0:8, :] = root
                    q[n, 0:8, :] = root * low
                    root = jnp.sqrt(jnp.where(row < 3, pltpu.roll(high, 3, 0), 0.0))
                    s[n, 72:80, :] = root
                    q[n, 72:80, :] = root * high
                for t in range(CY // 8):
                    root = jnp.sqrt(wide[HALO + plane, 8 * t : 8 * t + 8, lanes])
                    s[n, 8 * t + 8 : 8 * t + 16, :] = root
                    q[n, 8 * t + 8 : 8 * t + 16, :] = root * wide[plane, 8 * t : 8 * t + 8, lanes]

        def first(x, carry):
            for r in stretch(6, 74):
                root, sums = around(s, x, x - 1, x + 1, r, lane)
                centre, total = around(q, x, x - 1, x + 1, r, lane)
                for i in range(CHUNKS):
                    scaled = conductance * root[i]
                    keep = 1.0 - scaled * sums[i]
                    a[x * CHUNKS + i, pl.ds(r, 8), :] = keep
                    q1[x * CHUNKS + i, pl.ds(r, 8), :] = keep * centre[i] + (scaled * root[i]) * total[i]
            return carry

        lax.fori_loop(1, 4, first, 0)

        def second(x, carry):
            for r in stretch(7, 73):
                centre, total = around(q1, x, x - 1, x + 1, r, lane)
                for i in range(CHUNKS):
                    root = s[x * CHUNKS + i, pl.ds(r, 8), :]
                    keep = a[x * CHUNKS + i, pl.ds(r, 8), :]
                    q2[x * CHUNKS + i, pl.ds(r, 8), :] = keep * centre[i] + (conductance * root * root) * total[i]
            return carry

        lax.fori_loop(2, 5, second, 0)

        def third(x, carry):
            position = x - 3 if side == 0 else CX + 2 - x
            for r in stretch(8, 72):
                centre, total = around(q2, x, x - 1, x + 1, r, lane)
                for i in range(CHUNKS):
                    root = s[x * CHUNKS + i, pl.ds(r, 8), :]
                    keep = a[x * CHUNKS + i, pl.ds(r, 8), :]
                    full[position, pl.ds(r - 8, 8), pl.ds(LANES * i, LANES)] = (
                        keep * centre[i] / root + (conductance * root) * total[i]
                    )
            return carry

        lax.fori_loop(3, 6, third, 0)
        planes = pl.ds(0 if side == 0 else CX - HALO, HALO)
        store = pltpu.make_async_copy(full.at[planes], out.at[planes], sems.at[2 + side])
        store.start()
        stores.append(store)
    ask.wait()
    fill.wait()

    def answer(d, carry):
        value = zero
        for c in range(3):
            cell = asked[d, c]
            x, y, z = cell >> 15, (cell >> 9) & 63, cell & 511
            lanes = pl.ds(pl.multiple_of((z >> 7) * LANES, LANES), LANES)
            tile = full[x, pl.ds(pl.multiple_of((y >> 3) * 8, 8), 8), lanes]
            tile = pltpu.roll(tile, (LANES + c - (z & 127)) & 127, 1)
            value = jnp.where(jnp.logical_and(row == (y & 7), lane == c), tile, value)
        answers[pl.ds(d, 1), :] = jnp.sum(value, axis=0, keepdims=True)
        return carry

    lax.fori_loop(0, NGX, answer, 0, unroll=4)
    for store in stores:
        store.wait()


def outer(field, edges, x_up, x_down, c_up, c_down, cells):
    return pl.pallas_call(
        outer_kernel,
        out_shape=(shape(CX, CY, NZ), shape(NGX, LANES)),
        in_specs=[spec(ANY)] + [spec()] * 9 + [spec(ANY)],
        out_specs=(spec(ANY), spec()),
        scratch_shapes=[block(6), block(5), block(6), block(6), block(7)]
        + [
            VMEM((CX, CY, NZ), F32),
            pltpu.SMEM((NGX, LANES), jnp.int32),
            pltpu.SemaphoreType.DMA((4,)),
        ],
        input_output_aliases={0: 0},
        compiler_params=pltpu.CompilerParams(vmem_limit_bytes=32 << 20),
        name="outer",
    )(field, *edges, x_up, x_down, c_up, c_down, cells)


def friction_kernel(
    rates, answers, slip, aging, normal, shear, direct, evolution, distance, owner_row, owner_column, state_out, rate_out
):
    owners = owner_row[...]
    rank = rank_row(owners, owner_column[...])
    got = answers[...]
    named = lax.broadcasted_iota(jnp.int32, (NGX, TRI), 0) == owners
    held = jnp.zeros((NGX, TRI), F32)
    for c in range(3):
        held = jnp.where(jnp.logical_and(named, rank == float(c)), got[:, c : c + 1], held)
    pressure = jnp.sum(held, axis=0, keepdims=True)
    both = jnp.sum(rates[...], axis=0, keepdims=True)
    first, second = both[:, 0:TRI], both[:, TRI : 2 * TRI]
    effective = normal[...] + step_time * second - pressure
    ratio = distance[...] / slip[...]
    state = ratio + (aging[...] - ratio) * jnp.exp(-heal_time / ratio)
    state_out[...] = state
    rate_out[...] = (
        (shear[...] + step_time * first) / effective - friction_ref - evolution[...] * jnp.log(state / distance[...])
    ) / direct[...]


def friction(*values):
    return pl.pallas_call(
        friction_kernel,
        out_shape=(shape(1, TRI), shape(1, TRI)),
        in_specs=[spec()] * len(values),
        out_specs=(spec(), spec()),
        name="friction",
    )(*values)


def exchanged(value, axis):
    return lax.all_to_all(value, axis, split_axis=0, concat_axis=0, tiled=True)


def local(
    pressure,
    permeability,
    kernel,
    slip_rate,
    aging_state,
    normal_stress,
    shear_stress,
    direct_effect,
    evolution_effect,
    slip_distance,
    tri_owner,
    tri_cell,
):
    owner_row, cell_row = tri_owner.reshape(1, TRI), tri_cell.reshape(1, TRI)
    moved = lax.ppermute(slip_rate, ("gx", "gy"), SLIP_MOVES)
    x_up, x_down, y_up, y_down = pack(pressure, permeability)
    x_up, x_down = lax.ppermute(x_up, "gx", X_UP), lax.ppermute(x_down, "gx", X_DOWN)
    y_up, y_down = lax.ppermute(y_up, "gy", Y_UP), lax.ppermute(y_down, "gy", Y_DOWN)
    wanted = requests_of(owner_row, tri_owner, cell_row)
    lane = lax.broadcasted_iota(jnp.int32, (NGX, LANES), 1)
    row = jnp.pad(moved, (0, LANES - TRI)).reshape(1, LANES)
    arrived = exchanged(jnp.where(lane < TRI, row, wanted), "gx")
    partial_sums, cells = partial_rates(arrived, kernel)
    rates = exchanged(partial_sums, "gy")
    c_up = lax.ppermute(jnp.concatenate([y_up[CX - 2 :], y_down[CX - 2 :]]), "gx", X_UP)
    c_down = lax.ppermute(jnp.concatenate([y_up[:2], y_down[:2]]), "gx", X_DOWN)
    field, *edges = inner(pressure, permeability, y_up, y_down)
    field, answers = outer(field, edges, x_up, x_down, c_up, c_down, cells)
    answers = exchanged(answers, "gx")
    flat = [
        v.reshape(1, TRI)
        for v in (slip_rate, aging_state, normal_stress, shear_stress, direct_effect, evolution_effect, slip_distance)
    ]
    state_next, log_rate = friction(rates, answers, *flat, owner_row, tri_owner)
    return field, state_next.reshape(TRI), log_rate.reshape(TRI)


def solution(mesh):
    both = P(("gx", "gy"))
    placed = (
        P("gx", "gy", None),
        P("gx", "gy", None),
        P(None, "gx", "gy"),
        *([both] * 7),
        P(("gx", "gy"), None),
        both,
    )
    return jax.shard_map(
        local,
        mesh=mesh,
        in_specs=placed,
        out_specs=(P("gx", "gy", None), both, both),
        check_vma=False,
    )
```

```python
import jax
import jax.numpy as jnp
from jax import lax
from jax.experimental import pallas as pl
from jax.experimental.pallas import tpu as pltpu
from jax.sharding import PartitionSpec as P

NGX, NGY = 32, 8
CX, CY, NZ, TRI = 16, 64, 512, 48
HALO = 3
ROWS = 80
LANES = 128
CHUNKS = NZ // LANES
conductance = 0.15
step_time = 1.0
heal_time = 0.5
friction_ref = 0.6
F32 = jnp.float32
VMEM = pltpu.VMEM
ANY = pl.ANY

X_MOVE = (2, 1, 2, 1, 0, 3, 0, 3)
Y_MOVE = (1, 1, 0, 0, 0, 0, 1, 1)
X_CODE = sum(v << (2 * i) for i, v in enumerate(X_MOVE))
Y_CODE = sum(v << i for i, v in enumerate(Y_MOVE))


def landing(group, other):
    delta = (other - group) & 7
    x = ((group >> 1) + ((X_CODE >> (2 * delta)) & 3)) & 3
    y = (group & 1) ^ ((Y_CODE >> delta) & 1)
    return 2 * x + y


SLIP_MOVES = [
    ((4 * g + r) * NGY + j, (4 * landing(g, j) + r) * NGY + g) for g in range(8) for r in range(4) for j in range(NGY)
]
X_UP = [(i, i + 1) for i in range(NGX - 1)]
X_DOWN = [(j, i) for i, j in X_UP]
Y_UP = [(i, i + 1) for i in range(NGY - 1)]
Y_DOWN = [(j, i) for i, j in Y_UP]


def spec(space=VMEM):
    return pl.BlockSpec(memory_space=space)


def shape(*dims, dtype=F32):
    return jax.ShapeDtypeStruct(dims, dtype)


def far(value):
    return pltpu.with_memory_space_constraint(value, pltpu.HBM)


def all_far(*values):
    return tuple(far(v) for v in values)


def started(*copies):
    for copy in copies:
        copy.start()
    return copies


def waited(copies):
    for copy in copies:
        copy.wait()


HBM = pltpu.HBM
DMA = pltpu.SemaphoreType.DMA


def turned(row_value):
    row = lax.broadcasted_iota(jnp.int32, (TRI, TRI), 0)
    column = lax.broadcasted_iota(jnp.int32, (TRI, TRI), 1)
    return jnp.sum(jnp.where(row == column, row_value, 0.0), axis=1, keepdims=True)


def prepare_kernel(p, k, owner, cell, *refs):
    floats, (y_up, y_down, wanted, terms, tiles, whole, held, sems) = refs[:7], refs[7:]
    tops = started(
        pltpu.make_async_copy(p.at[:, pl.ds(CY - 8, 8), :], tiles.at[0], sems.at[0]),
        pltpu.make_async_copy(k.at[:, pl.ds(CY - 8, 8), :], tiles.at[1], sems.at[1]),
        pltpu.make_async_copy(p.at[:, pl.ds(0, 8), :], tiles.at[2], sems.at[2]),
        pltpu.make_async_copy(k.at[:, pl.ds(0, 8), :], tiles.at[3], sems.at[3]),
    )
    small = started(
        pltpu.make_async_copy(owner, whole.at[0], sems.at[4]),
        pltpu.make_async_copy(cell, whole.at[1], sems.at[5]),
        *[pltpu.make_async_copy(ref, held.at[n], sems.at[6 + n]) for n, ref in enumerate(floats)],
    )
    waited(small)
    slip, aging, normal, shear, direct, evolution, distance = (held[n] for n in range(7))
    owners = whole[0].astype(F32)
    first = lax.broadcasted_iota(jnp.int32, (TRI, TRI), 0)
    second = lax.broadcasted_iota(jnp.int32, (TRI, TRI), 1)
    same = jnp.logical_and(turned(owners) == owners, first < second)
    rank = jnp.sum(jnp.where(same, 1.0, 0.0), axis=0, keepdims=True)
    cells = whole[1].astype(F32)
    lane = lax.broadcasted_iota(jnp.int32, (NGX, LANES), 1)
    named = lax.broadcasted_iota(jnp.int32, (NGX, TRI), 0) == whole[0]
    value = jnp.zeros((NGX, LANES), F32)
    for c in range(3):
        asked = jnp.where(jnp.logical_and(named, rank == float(c)), cells, 0.0)
        value = jnp.where(lane == TRI + c, jnp.sum(asked, axis=1, keepdims=True), value)
    wanted[...] = value
    ratio = distance / slip
    state = ratio + (aging - ratio) * jnp.exp(-heal_time / ratio)
    terms[...] = jnp.zeros((8, LANES), F32)
    aged = evolution * jnp.log(state / distance)
    for n, term in enumerate((state, aged, normal, shear, direct, owners, rank)):
        terms[n : n + 1, 0:TRI] = term
    waited(tops)
    row = lax.broadcasted_iota(jnp.int32, (8, NZ), 0)

    def plane(x, carry):
        y_up[x] = jnp.where(row >= 5, tiles[0, x], pltpu.roll(tiles[1, x], 3, 0))
        y_down[x] = jnp.where(row < 3, tiles[2, x], pltpu.roll(tiles[3, x], 5, 0))
        return carry

    lax.fori_loop(0, CX, plane, 0)


def prepare(*values):
    return pl.pallas_call(
        prepare_kernel,
        out_shape=(
            shape(CX, 8, NZ),
            shape(CX, 8, NZ),
            shape(NGX, LANES),
            shape(8, LANES),
        ),
        in_specs=[spec(HBM)] * len(values),
        out_specs=(spec(),) * 4,
        scratch_shapes=[VMEM((4, CX, 8, NZ), F32), VMEM((2, 1, TRI), jnp.int32), VMEM((7, 1, TRI), F32), DMA((13,))],
        compiler_params=pltpu.CompilerParams(vmem_limit_bytes=4 << 20),
        name="prepare",
    )(*all_far(*values))


def halo_rows(low, high, row):
    p = jnp.where(row >= 5, low, jnp.where(row < 3, high, 0.0))
    k = jnp.where(row >= 5, pltpu.roll(low, 5, 0), jnp.where(row < 3, pltpu.roll(high, 3, 0), 0.0))
    return p, k


def sides_kernel(p, k, y_up, y_down, token, x_up, x_down, sems):
    del token
    copies = []
    for side, (target, start) in enumerate(((x_up, CX - HALO), (x_down, 0))):
        for n, source in enumerate((p, k)):
            copies.append(
                pltpu.make_async_copy(
                    source.at[pl.ds(start, HALO)], target.at[pl.ds(HALO * n, HALO), pl.ds(0, CY)], sems.at[2 * side + n]
                )
            )
    started(*copies)
    row = lax.broadcasted_iota(jnp.int32, (8, NZ), 0)
    for target, start in ((x_up, CX - HALO), (x_down, 0)):
        for n in range(HALO):
            halo_p, halo_k = halo_rows(y_up[start + n], y_down[start + n], row)
            target[n, CY : CY + 8, :] = halo_p
            target[HALO + n, CY : CY + 8, :] = halo_k
    waited(copies)


def sides(p, k, y_up, y_down, token):
    return pl.pallas_call(
        sides_kernel,
        out_shape=(shape(2 * HALO, CY + 8, NZ),) * 2,
        in_specs=[spec(HBM)] * 2 + [spec()] * 2 + [spec(ANY)],
        out_specs=(spec(),) * 2,
        scratch_shapes=[DMA((4,))],
        compiler_params=pltpu.CompilerParams(vmem_limit_bytes=4 << 20),
        name="sides",
    )(far(p), far(k), y_up, y_down, token)


def rates_kernel(arrived, kernel_far, token, out, cells, acc, kernel, sems):
    del token
    copies = started(
        *[
            pltpu.make_async_copy(
                kernel_far.at[n // 4, pl.ds(96 * (n % 4), 96)], kernel.at[n // 4, pl.ds(96 * (n % 4), 96)], sems.at[n]
            )
            for n in range(8)
        ]
    )
    gy = lax.axis_index("gy")
    lane = lax.broadcasted_iota(jnp.int32, (1, LANES), 1)
    chunks = [jnp.zeros((1, LANES), F32) for _ in range(12)]
    for j in range(NGY):
        spot = landing(gy, j)
        for r in range(4):
            start = (r * NGY + j) * TRI
            chunk, offset = divmod(start, LANES)
            row = pltpu.roll(arrived[pl.ds(4 * spot + r, 1), :], offset, 1)
            inside = jnp.logical_and(lane >= offset, lane < offset + TRI)
            chunks[chunk] = jnp.where(inside, row, chunks[chunk])
            if offset + TRI > LANES:
                chunks[chunk + 1] = jnp.where(lane < offset + TRI - LANES, row, chunks[chunk + 1])
    cells[...] = pltpu.roll(arrived[...], LANES - TRI, 1).astype(jnp.int32)
    wide = [jnp.broadcast_to(c, (8, LANES)) for c in chunks]

    for n in range(8):
        part = n // 4
        copies[n].wait()

        def tile(t, carry):
            rows = pl.ds(pl.multiple_of(t * 8, 8), 8)
            terms = [kernel[part, rows, pl.ds(LANES * c, LANES)] * wide[c] for c in range(12)]
            while len(terms) > 1:
                terms = [a + b for a, b in zip(terms[::2], terms[1::2])] + terms[len(terms) // 2 * 2 :]
            dest = (t // 6) * 96 + part * TRI + (t % 6) * 8
            acc[pl.ds(pl.multiple_of(dest, 8), 8), :] = terms[0]
            return carry

        lax.fori_loop(12 * (n % 4), 12 * (n % 4) + 12, tile, 0, unroll=4)
    row8 = lax.broadcasted_iota(jnp.int32, (8, LANES), 0)
    total = jnp.zeros((8, 2 * TRI), F32)
    for j in range(NGY):
        total = total + lax.dot_general(
            jnp.where(row8 == j, 1.0, 0.0),
            acc[pl.ds(2 * TRI * j, 2 * TRI), :],
            (((1,), (1,)), ((), ())),
            precision=lax.Precision.HIGHEST,
            preferred_element_type=F32,
        )
    out[...] = jnp.zeros((8, LANES), F32)
    out[:, 0 : 2 * TRI] = total


def partial_rates(arrived, kernel, token):
    return pl.pallas_call(
        rates_kernel,
        out_shape=(shape(NGY, LANES), shape(NGX, LANES, dtype=jnp.int32)),
        in_specs=[spec(), spec(HBM), spec(ANY)],
        out_specs=(spec(), spec()),
        scratch_shapes=[VMEM((768, LANES), F32), VMEM(kernel.shape, F32), DMA((8,))],
        compiler_params=pltpu.CompilerParams(vmem_limit_bytes=8 << 20),
        name="rates",
    )(arrived, far(kernel), token)


def around(ref, x, before, after, row, lane):
    rows = pl.ds(row, 8)
    centre = [ref[x * CHUNKS + i, rows, :] for i in range(CHUNKS)]
    left = [pltpu.roll(v, 1, 1) for v in centre]
    right = [pltpu.roll(v, LANES - 1, 1) for v in centre]
    sums = []
    for i in range(CHUNKS):
        below = left[i - 1] if i else 0.0
        above = right[i + 1] if i + 1 < CHUNKS else 0.0
        z = jnp.where(lane == 0, below, left[i]) + jnp.where(lane == LANES - 1, above, right[i])
        y = ref[x * CHUNKS + i, pl.ds(row - 1, 8), :] + ref[x * CHUNKS + i, pl.ds(row + 1, 8), :]
        xs = ref[before * CHUNKS + i, rows, :] + ref[after * CHUNKS + i, rows, :]
        sums.append((xs + y) + z)
    return centre, sums


def stretch(first, last):
    return range(first, last, 8)


EDGES = ((3, 3), (2, 3), (2, 4), (2, 4), (2, 5))


def edge_copies(which, source, edge, sems):
    count, depth = EDGES[which]
    copies = []
    for n in range(count):
        inside = depth - HALO + n
        for side, x in enumerate((inside, CX - 1 - inside)):
            copies.append(
                pltpu.make_async_copy(
                    source.at[pl.ds(x * CHUNKS, CHUNKS)], edge.at[side, pl.ds(n * CHUNKS, CHUNKS)], sems.at[2 * n + side]
                )
            )
    return started(*copies)


def inner_kernel(
    p_far, k_far, y_up, y_down, token, out, s_edge, q_edge, a_edge, q1_edge, q2_edge, s, q, a, q1, q2, p, k, field, sems, edge_sems
):
    del token
    loads = [
        started(
            pltpu.make_async_copy(p_far.at[pl.ds(4 * n, 4)], p.at[pl.ds(4 * n, 4)], sems.at[2 * n]),
            pltpu.make_async_copy(k_far.at[pl.ds(4 * n, 4)], k.at[pl.ds(4 * n, 4)], sems.at[2 * n + 1]),
        )
        for n in range(4)
    ]
    edges = []
    lane = lax.broadcasted_iota(jnp.int32, (8, LANES), 1)
    row = lax.broadcasted_iota(jnp.int32, (8, LANES), 0)

    def convert(x, carry):
        for i in range(CHUNKS):
            lanes = pl.ds(LANES * i, LANES)
            n = x * CHUNKS + i
            halo_p, halo_k = halo_rows(y_up[x, :, lanes], y_down[x, :, lanes], row)
            root = jnp.sqrt(halo_k)
            scaled = root * halo_p
            for place in (0, CY + 8):
                s[n, place : place + 8, :] = root
                q[n, place : place + 8, :] = scaled
            for t in range(CY // 8):
                root = jnp.sqrt(k[x, 8 * t : 8 * t + 8, lanes])
                s[n, 8 * t + 8 : 8 * t + 16, :] = root
                q[n, 8 * t + 8 : 8 * t + 16, :] = root * p[x, 8 * t : 8 * t + 8, lanes]
        return carry

    for n in range(4):
        waited(loads[n])
        lax.fori_loop(4 * n, 4 * n + 4, convert, 0)
    edges += edge_copies(0, s, s_edge, edge_sems.at[0])
    edges += edge_copies(1, q, q_edge, edge_sems.at[1])

    def first(x, carry):
        for r in stretch(6, 74):
            root, sums = around(s, x, x - 1, x + 1, r, lane)
            centre, total = around(q, x, x - 1, x + 1, r, lane)
            for i in range(CHUNKS):
                scaled = conductance * root[i]
                keep = 1.0 - scaled * sums[i]
                a[x * CHUNKS + i, pl.ds(r, 8), :] = keep
                q1[x * CHUNKS + i, pl.ds(r, 8), :] = keep * centre[i] + (scaled * root[i]) * total[i]
        return carry

    lax.fori_loop(1, CX - 1, first, 0)
    edges += edge_copies(2, a, a_edge, edge_sems.at[2])
    edges += edge_copies(3, q1, q1_edge, edge_sems.at[3])

    def second(x, carry):
        for r in stretch(7, 73):
            centre, total = around(q1, x, x - 1, x + 1, r, lane)
            for i in range(CHUNKS):
                root = s[x * CHUNKS + i, pl.ds(r, 8), :]
                keep = a[x * CHUNKS + i, pl.ds(r, 8), :]
                q2[x * CHUNKS + i, pl.ds(r, 8), :] = keep * centre[i] + (conductance * root * root) * total[i]
        return carry

    lax.fori_loop(2, CX - 2, second, 0)
    edges += edge_copies(4, q2, q2_edge, edge_sems.at[4])

    def third(x, carry):
        for r in stretch(8, 72):
            centre, total = around(q2, x, x - 1, x + 1, r, lane)
            for i in range(CHUNKS):
                root = s[x * CHUNKS + i, pl.ds(r, 8), :]
                keep = a[x * CHUNKS + i, pl.ds(r, 8), :]
                field[x - HALO, pl.ds(r - 8, 8), pl.ds(LANES * i, LANES)] = (
                    keep * centre[i] / root + (conductance * root) * total[i]
                )
        return carry

    for n in range(2):
        start = HALO + 5 * n
        lax.fori_loop(start, start + 5, third, 0)
        edges += started(
            pltpu.make_async_copy(field.at[pl.ds(5 * n, 5)], out.at[pl.ds(start, 5)], sems.at[8 + n])
        )
    waited(edges)


def block(planes):
    return VMEM((planes * CHUNKS, ROWS, LANES), F32)


def inner(p, k, y_up, y_down, token):
    return pl.pallas_call(
        inner_kernel,
        out_shape=(shape(CX, CY, NZ),) + tuple(shape(2, n * CHUNKS, ROWS, LANES) for n, _ in EDGES),
        in_specs=[spec(HBM)] * 2 + [spec()] * 2 + [spec(ANY)],
        out_specs=(spec(HBM),) * 6,
        scratch_shapes=[block(CX) for _ in range(5)]
        + [VMEM((CX, CY, NZ), F32), VMEM((CX, CY, NZ), F32), VMEM((CX - 2 * HALO, CY, NZ), F32), DMA((10,)), DMA((5, 6))],
        compiler_params=pltpu.CompilerParams(vmem_limit_bytes=24 << 20),
        cost_estimate=pl.CostEstimate(flops=40_000_000, bytes_accessed=12_000_000, transcendentals=0),
        name="inner",
    )(far(p), far(k), y_up, y_down, token)


def outer_kernel(
    field, s_edge, q_edge, a_edge, q1_edge, q2_edge, x_up, x_down, cells, out, answers, s, q, a, q1, q2, full, asked, sems, edge_sems
):
    del field
    loads = [[], []]
    for side in range(2):
        for n, (edge, target) in enumerate(zip((s_edge, q_edge, a_edge, q1_edge, q2_edge), (s, q, a, q1, q2))):
            count, depth = EDGES[n]
            loads[side] += started(
                pltpu.make_async_copy(
                    edge.at[side], target.at[side, pl.ds(depth * CHUNKS, count * CHUNKS)], edge_sems.at[side, n]
                )
            )
    ask = pltpu.make_async_copy(cells, asked, sems.at[0])
    ask.start()
    fill = pltpu.make_async_copy(
        out.at[pl.ds(HALO, CX - 2 * HALO)], full.at[pl.ds(HALO, CX - 2 * HALO)], sems.at[1]
    )
    fill.start()
    lane = lax.broadcasted_iota(jnp.int32, (8, LANES), 1)
    row = lax.broadcasted_iota(jnp.int32, (8, LANES), 0)
    zero = jnp.zeros((8, LANES), F32)
    stores = []
    both = (s, q, a, q1, q2)
    for side, wide in enumerate((x_up, x_down)):
        s, q, a, q1, q2 = (ref.at[side] for ref in both)
        for d in range(HALO):
            plane = d if side == 0 else HALO - 1 - d
            for i in range(CHUNKS):
                lanes = pl.ds(LANES * i, LANES)
                n = d * CHUNKS + i
                for t in range(CY // 8 + 1):
                    root = jnp.sqrt(wide[HALO + plane, 8 * t : 8 * t + 8, lanes])
                    scaled = root * wide[plane, 8 * t : 8 * t + 8, lanes]
                    for place in (8 * t + 8,) if t < CY // 8 else (0, CY + 8):
                        s[n, place : place + 8, :] = root
                        q[n, place : place + 8, :] = scaled
        waited(loads[side])

        def first(x, carry):
            for r in stretch(6, 74):
                root, sums = around(s, x, x - 1, x + 1, r, lane)
                centre, total = around(q, x, x - 1, x + 1, r, lane)
                for i in range(CHUNKS):
                    scaled = conductance * root[i]
                    keep = 1.0 - scaled * sums[i]
                    a[x * CHUNKS + i, pl.ds(r, 8), :] = keep
                    q1[x * CHUNKS + i, pl.ds(r, 8), :] = keep * centre[i] + (scaled * root[i]) * total[i]
            return carry

        lax.fori_loop(1, 4, first, 0)

        def second(x, carry):
            for r in stretch(7, 73):
                centre, total = around(q1, x, x - 1, x + 1, r, lane)
                for i in range(CHUNKS):
                    root = s[x * CHUNKS + i, pl.ds(r, 8), :]
                    keep = a[x * CHUNKS + i, pl.ds(r, 8), :]
                    q2[x * CHUNKS + i, pl.ds(r, 8), :] = keep * centre[i] + (conductance * root * root) * total[i]
            return carry

        lax.fori_loop(2, 5, second, 0)

        def third(x, carry):
            position = x - 3 if side == 0 else CX + 2 - x
            for r in stretch(8, 72):
                centre, total = around(q2, x, x - 1, x + 1, r, lane)
                for i in range(CHUNKS):
                    root = s[x * CHUNKS + i, pl.ds(r, 8), :]
                    keep = a[x * CHUNKS + i, pl.ds(r, 8), :]
                    full[position, pl.ds(r - 8, 8), pl.ds(LANES * i, LANES)] = (
                        keep * centre[i] / root + (conductance * root) * total[i]
                    )
            return carry

        lax.fori_loop(3, 6, third, 0)
        planes = pl.ds(0 if side == 0 else CX - HALO, HALO)
        store = pltpu.make_async_copy(full.at[planes], out.at[planes], sems.at[2 + side])
        store.start()
        stores.append(store)
    ask.wait()
    fill.wait()

    def answer(d, carry):
        value = zero
        for c in range(3):
            cell = asked[d, c]
            x, y, z = cell >> 15, (cell >> 9) & 63, cell & 511
            lanes = pl.ds(pl.multiple_of((z >> 7) * LANES, LANES), LANES)
            tile = full[x, pl.ds(pl.multiple_of((y >> 3) * 8, 8), 8), lanes]
            tile = pltpu.roll(tile, (LANES + c - (z & 127)) & 127, 1)
            value = jnp.where(jnp.logical_and(row == (y & 7), lane == c), tile, value)
        answers[pl.ds(d, 1), :] = jnp.sum(value, axis=0, keepdims=True)
        return carry

    lax.fori_loop(0, NGX, answer, 0, unroll=4)
    for store in stores:
        store.wait()


def outer(field, edges, x_up, x_down, cells):
    return pl.pallas_call(
        outer_kernel,
        out_shape=(shape(CX, CY, NZ), shape(NGX, LANES)),
        in_specs=[spec(HBM)] * 6 + [spec()] * 2 + [spec(ANY)],
        out_specs=(spec(pltpu.HBM), spec()),
        scratch_shapes=[VMEM((2, n * CHUNKS, ROWS, LANES), F32) for n in (6, 5, 6, 6, 7)]
        + [
            VMEM((CX, CY, NZ), F32),
            pltpu.SMEM((NGX, LANES), jnp.int32),
            DMA((4,)),
            DMA((2, 5)),
        ],
        input_output_aliases={0: 0},
        compiler_params=pltpu.CompilerParams(vmem_limit_bytes=20 << 20),
        name="outer",
    )(field, *edges, x_up, x_down, cells)


def friction_kernel(rates, answers, terms, state_out, rate_out):
    known = terms[...]
    state, aged, normal, shear, direct, owners, rank = (known[i : i + 1, 0:TRI] for i in range(7))
    got = answers[...]
    named = lax.broadcasted_iota(jnp.int32, (NGX, TRI), 0).astype(F32) == owners
    held = jnp.zeros((NGX, TRI), F32)
    for c in range(3):
        held = jnp.where(jnp.logical_and(named, rank == float(c)), got[:, c : c + 1], held)
    pressure = jnp.sum(held, axis=0, keepdims=True)
    both = jnp.sum(rates[...], axis=0, keepdims=True)
    first, second = both[:, 0:TRI], both[:, TRI : 2 * TRI]
    effective = normal + step_time * second - pressure
    state_out[...] = state
    rate_out[...] = ((shear + step_time * first) / effective - friction_ref - aged) / direct


def friction(*values):
    return pl.pallas_call(
        friction_kernel,
        out_shape=(shape(1, TRI), shape(1, TRI)),
        in_specs=[spec()] * len(values),
        out_specs=(spec(), spec()),
        compiler_params=pltpu.CompilerParams(vmem_limit_bytes=4 << 20),
        name="friction",
    )(*values)


def exchanged(value, axis):
    return lax.all_to_all(value, axis, split_axis=0, concat_axis=0, tiled=True)


def local(
    pressure,
    permeability,
    kernel,
    slip_rate,
    aging_state,
    normal_stress,
    shear_stress,
    direct_effect,
    evolution_effect,
    slip_distance,
    tri_owner,
    tri_cell,
):
    moved = lax.ppermute(slip_rate, ("gx", "gy"), SLIP_MOVES)
    rows = (
        tri_owner,
        tri_cell,
        slip_rate,
        aging_state,
        normal_stress,
        shear_stress,
        direct_effect,
        evolution_effect,
        slip_distance,
    )
    y_up, y_down, wanted, terms = prepare(pressure, permeability, *[v.reshape(1, TRI) for v in rows])
    y_up, y_down = lax.ppermute(y_up, "gy", Y_UP), lax.ppermute(y_down, "gy", Y_DOWN)
    lane = lax.broadcasted_iota(jnp.int32, (NGX, LANES), 1)
    row = jnp.pad(moved, (0, LANES - TRI)).reshape(1, LANES)
    leaving = jnp.where(lane < TRI, row, wanted)
    arrived = exchanged(leaving, "gx")
    x_up, x_down = sides(pressure, permeability, y_up, y_down, leaving)
    field, *edges = inner(pressure, permeability, y_up, y_down, x_up)
    x_up, x_down = lax.ppermute(x_up, "gx", X_UP), lax.ppermute(x_down, "gx", X_DOWN)
    partial_sums, cells = partial_rates(arrived, kernel, edges[1])
    rates = exchanged(partial_sums, "gy")
    field, answers = outer(field, edges, x_up, x_down, cells)
    answers = exchanged(answers, "gx")
    state_next, log_rate = friction(rates, answers, terms)
    return field, state_next.reshape(TRI), log_rate.reshape(TRI)


def solution(mesh):
    both = P(("gx", "gy"))
    placed = (
        P("gx", "gy", None),
        P("gx", "gy", None),
        P(None, "gx", "gy"),
        *([both] * 7),
        P(("gx", "gy"), None),
        both,
    )
    return jax.shard_map(
        local,
        mesh=mesh,
        in_specs=placed,
        out_specs=(P("gx", "gy", None), both, both),
        check_vma=False,
    )
```

```python
import jax
import jax.numpy as jnp
from jax import lax
from jax.experimental import pallas as pl
from jax.experimental.pallas import tpu as pltpu
from jax.sharding import PartitionSpec as P

NGX, NGY = 32, 8
CX, CY, NZ, TRI = 16, 64, 512, 48
HALO = 3
ROWS = 80
LANES = 128
CHUNKS = NZ // LANES
conductance = 0.15
step_time = 1.0
heal_time = 0.5
friction_ref = 0.6
F32 = jnp.float32
VMEM = pltpu.VMEM
ANY = pl.ANY

X_MOVE = (2, 1, 2, 1, 0, 3, 0, 3)
Y_MOVE = (1, 1, 0, 0, 0, 0, 1, 1)
X_CODE = sum(v << (2 * i) for i, v in enumerate(X_MOVE))
Y_CODE = sum(v << i for i, v in enumerate(Y_MOVE))


def landing(group, other):
    delta = (other - group) & 7
    x = ((group >> 1) + ((X_CODE >> (2 * delta)) & 3)) & 3
    y = (group & 1) ^ ((Y_CODE >> delta) & 1)
    return 2 * x + y


SLIP_MOVES = [
    ((4 * g + r) * NGY + j, (4 * landing(g, j) + r) * NGY + g) for g in range(8) for r in range(4) for j in range(NGY)
]
X_UP = [(i, i + 1) for i in range(NGX - 1)]
X_DOWN = [(j, i) for i, j in X_UP]
Y_UP = [(i, i + 1) for i in range(NGY - 1)]
Y_DOWN = [(j, i) for i, j in Y_UP]


def spec(space=VMEM):
    return pl.BlockSpec(memory_space=space)


def shape(*dims, dtype=F32):
    return jax.ShapeDtypeStruct(dims, dtype)


def far(value):
    return pltpu.with_memory_space_constraint(value, pltpu.HBM)


def all_far(*values):
    return tuple(far(v) for v in values)


def started(*copies):
    for copy in copies:
        copy.start()
    return copies


def waited(copies):
    for copy in copies:
        copy.wait()


HBM = pltpu.HBM
DMA = pltpu.SemaphoreType.DMA


def turned(row_value):
    row = lax.broadcasted_iota(jnp.int32, (TRI, TRI), 0)
    column = lax.broadcasted_iota(jnp.int32, (TRI, TRI), 1)
    return jnp.sum(jnp.where(row == column, row_value, 0.0), axis=1, keepdims=True)


def pack_kernel(p, k, y_up, y_down, tiles, sems):
    tops = started(
        pltpu.make_async_copy(p.at[:, pl.ds(CY - 8, 8), :], tiles.at[0], sems.at[0]),
        pltpu.make_async_copy(k.at[:, pl.ds(CY - 8, 8), :], tiles.at[1], sems.at[1]),
        pltpu.make_async_copy(p.at[:, pl.ds(0, 8), :], tiles.at[2], sems.at[2]),
        pltpu.make_async_copy(k.at[:, pl.ds(0, 8), :], tiles.at[3], sems.at[3]),
    )
    row = lax.broadcasted_iota(jnp.int32, (8, NZ), 0)
    waited(tops)

    def plane(x, carry):
        y_up[x] = jnp.where(row >= 5, tiles[0, x], pltpu.roll(tiles[1, x], 3, 0))
        y_down[x] = jnp.where(row < 3, tiles[2, x], pltpu.roll(tiles[3, x], 5, 0))
        return carry

    lax.fori_loop(0, CX, plane, 0)


def pack(p, k):
    return pl.pallas_call(
        pack_kernel,
        out_shape=(shape(CX, 8, NZ),) * 2,
        in_specs=[spec(HBM)] * 2,
        out_specs=(spec(),) * 2,
        scratch_shapes=[VMEM((4, CX, 8, NZ), F32), DMA((4,))],
        compiler_params=pltpu.CompilerParams(vmem_limit_bytes=4 << 20),
        name="pack",
    )(far(p), far(k))


def prepare_kernel(owner, cell, *refs):
    floats, (wanted, terms, whole, held, sems) = refs[:7], refs[7:]
    waited(
        started(
            pltpu.make_async_copy(owner, whole.at[0], sems.at[0]),
            pltpu.make_async_copy(cell, whole.at[1], sems.at[1]),
            *[pltpu.make_async_copy(ref, held.at[n], sems.at[2 + n]) for n, ref in enumerate(floats)],
        )
    )
    slip, aging, normal, shear, direct, evolution, distance = (held[n] for n in range(7))
    owners = whole[0].astype(F32)
    first = lax.broadcasted_iota(jnp.int32, (TRI, TRI), 0)
    second = lax.broadcasted_iota(jnp.int32, (TRI, TRI), 1)
    same = jnp.logical_and(turned(owners) == owners, first < second)
    rank = jnp.sum(jnp.where(same, 1.0, 0.0), axis=0, keepdims=True)
    cells = whole[1].astype(F32)
    lane = lax.broadcasted_iota(jnp.int32, (NGX, LANES), 1)
    named = lax.broadcasted_iota(jnp.int32, (NGX, TRI), 0) == whole[0]
    value = jnp.zeros((NGX, LANES), F32)
    for c in range(3):
        asked = jnp.where(jnp.logical_and(named, rank == float(c)), cells, 0.0)
        value = jnp.where(lane == TRI + c, jnp.sum(asked, axis=1, keepdims=True), value)
    wanted[...] = value
    ratio = distance / slip
    state = ratio + (aging - ratio) * jnp.exp(-heal_time / ratio)
    terms[...] = jnp.zeros((8, LANES), F32)
    aged = evolution * jnp.log(state / distance)
    for n, term in enumerate((state, aged, normal, shear, direct, owners, rank)):
        terms[n : n + 1, 0:TRI] = term


def prepare(*values):
    return pl.pallas_call(
        prepare_kernel,
        out_shape=(shape(NGX, LANES), shape(8, LANES)),
        in_specs=[spec(HBM)] * len(values),
        out_specs=(spec(),) * 2,
        scratch_shapes=[VMEM((2, 1, TRI), jnp.int32), VMEM((7, 1, TRI), F32), DMA((9,))],
        compiler_params=pltpu.CompilerParams(vmem_limit_bytes=2 << 20),
        name="prepare",
    )(*all_far(*values))


def halo_rows(low, high, row):
    p = jnp.where(row >= 5, low, jnp.where(row < 3, high, 0.0))
    k = jnp.where(row >= 5, pltpu.roll(low, 5, 0), jnp.where(row < 3, pltpu.roll(high, 3, 0), 0.0))
    return p, k


def sides_kernel(p, k, y_up, y_down, token, x_up, x_down, sems):
    del token
    copies = []
    for side, (target, start) in enumerate(((x_up, CX - HALO), (x_down, 0))):
        for n, source in enumerate((p, k)):
            copies.append(
                pltpu.make_async_copy(
                    source.at[pl.ds(start, HALO)], target.at[pl.ds(HALO * n, HALO), pl.ds(0, CY)], sems.at[2 * side + n]
                )
            )
    started(*copies)
    row = lax.broadcasted_iota(jnp.int32, (8, NZ), 0)
    for target, start in ((x_up, CX - HALO), (x_down, 0)):
        for n in range(HALO):
            halo_p, halo_k = halo_rows(y_up[start + n], y_down[start + n], row)
            target[n, CY : CY + 8, :] = halo_p
            target[HALO + n, CY : CY + 8, :] = halo_k
    waited(copies)


def sides(p, k, y_up, y_down, token):
    return pl.pallas_call(
        sides_kernel,
        out_shape=(shape(2 * HALO, CY + 8, NZ),) * 2,
        in_specs=[spec(HBM)] * 2 + [spec()] * 2 + [spec(ANY)],
        out_specs=(spec(),) * 2,
        scratch_shapes=[DMA((4,))],
        compiler_params=pltpu.CompilerParams(vmem_limit_bytes=4 << 20),
        name="sides",
    )(far(p), far(k), y_up, y_down, token)


def rates_kernel(arrived, kernel_far, out, cells, acc, kernel, sems):
    copies = started(
        *[
            pltpu.make_async_copy(
                kernel_far.at[n // 4, pl.ds(96 * (n % 4), 96)], kernel.at[n // 4, pl.ds(96 * (n % 4), 96)], sems.at[n]
            )
            for n in range(8)
        ]
    )
    gy = lax.axis_index("gy")
    lane = lax.broadcasted_iota(jnp.int32, (1, LANES), 1)
    chunks = [jnp.zeros((1, LANES), F32) for _ in range(12)]
    for j in range(NGY):
        spot = landing(gy, j)
        for r in range(4):
            start = (r * NGY + j) * TRI
            chunk, offset = divmod(start, LANES)
            row = pltpu.roll(arrived[pl.ds(4 * spot + r, 1), :], offset, 1)
            inside = jnp.logical_and(lane >= offset, lane < offset + TRI)
            chunks[chunk] = jnp.where(inside, row, chunks[chunk])
            if offset + TRI > LANES:
                chunks[chunk + 1] = jnp.where(lane < offset + TRI - LANES, row, chunks[chunk + 1])
    cells[...] = pltpu.roll(arrived[...], LANES - TRI, 1).astype(jnp.int32)
    wide = [jnp.broadcast_to(c, (8, LANES)) for c in chunks]

    for n in range(8):
        part = n // 4
        copies[n].wait()

        def tile(t, carry):
            rows = pl.ds(pl.multiple_of(t * 8, 8), 8)
            terms = [kernel[part, rows, pl.ds(LANES * c, LANES)] * wide[c] for c in range(12)]
            while len(terms) > 1:
                terms = [a + b for a, b in zip(terms[::2], terms[1::2])] + terms[len(terms) // 2 * 2 :]
            dest = (t // 6) * 96 + part * TRI + (t % 6) * 8
            acc[pl.ds(pl.multiple_of(dest, 8), 8), :] = terms[0]
            return carry

        lax.fori_loop(12 * (n % 4), 12 * (n % 4) + 12, tile, 0, unroll=4)
    row8 = lax.broadcasted_iota(jnp.int32, (8, LANES), 0)
    total = jnp.zeros((8, 2 * TRI), F32)
    for j in range(NGY):
        total = total + lax.dot_general(
            jnp.where(row8 == j, 1.0, 0.0),
            acc[pl.ds(2 * TRI * j, 2 * TRI), :],
            (((1,), (1,)), ((), ())),
            precision=lax.Precision.HIGHEST,
            preferred_element_type=F32,
        )
    out[...] = jnp.zeros((8, LANES), F32)
    out[:, 0 : 2 * TRI] = total


def partial_rates(arrived, kernel):
    return pl.pallas_call(
        rates_kernel,
        out_shape=(shape(NGY, LANES), shape(NGX, LANES, dtype=jnp.int32)),
        in_specs=[spec(), spec(HBM)],
        out_specs=(spec(), spec()),
        scratch_shapes=[VMEM((768, LANES), F32), VMEM(kernel.shape, F32), DMA((8,))],
        compiler_params=pltpu.CompilerParams(vmem_limit_bytes=8 << 20),
        cost_estimate=pl.CostEstimate(flops=1000000000000, bytes_accessed=6000000000, transcendentals=0),
        name="rates",
    )(arrived, far(kernel))


def around(ref, x, before, after, row, lane):
    rows = pl.ds(row, 8)
    centre = [ref[x * CHUNKS + i, rows, :] for i in range(CHUNKS)]
    left = [pltpu.roll(v, 1, 1) for v in centre]
    right = [pltpu.roll(v, LANES - 1, 1) for v in centre]
    sums = []
    for i in range(CHUNKS):
        below = left[i - 1] if i else 0.0
        above = right[i + 1] if i + 1 < CHUNKS else 0.0
        z = jnp.where(lane == 0, below, left[i]) + jnp.where(lane == LANES - 1, above, right[i])
        y = ref[x * CHUNKS + i, pl.ds(row - 1, 8), :] + ref[x * CHUNKS + i, pl.ds(row + 1, 8), :]
        xs = ref[before * CHUNKS + i, rows, :] + ref[after * CHUNKS + i, rows, :]
        sums.append((xs + y) + z)
    return centre, sums


PLANES = CX + 2 * HALO


def diffusion_kernel(
    p_far, k_far, y_up, y_down, x_up, x_down, cells, out, answers, s, q, a, q1, q2, p, k, full, asked, sems
):
    loads = [
        started(
            pltpu.make_async_copy(p_far.at[pl.ds(4 * n, 4)], p.at[pl.ds(4 * n, 4)], sems.at[2 * n]),
            pltpu.make_async_copy(k_far.at[pl.ds(4 * n, 4)], k.at[pl.ds(4 * n, 4)], sems.at[2 * n + 1]),
        )
        for n in range(4)
    ]
    ask = started(pltpu.make_async_copy(cells, asked, sems.at[8]))
    lane = lax.broadcasted_iota(jnp.int32, (8, LANES), 1)
    row = lax.broadcasted_iota(jnp.int32, (8, LANES), 0)

    def put(n, places, p_tile, k_tile):
        root = jnp.sqrt(k_tile)
        scaled = root * p_tile
        for place in places:
            s[n, place : place + 8, :] = root
            q[n, place : place + 8, :] = scaled

    def outside(wide, base):
        def plane(n, carry):
            for i in range(CHUNKS):
                lanes = pl.ds(LANES * i, LANES)
                for t in range(CY // 8 + 1):
                    places = (8 * t + 8,) if t < CY // 8 else (0, CY + 8)
                    rows = pl.ds(8 * t, 8)
                    put((base + n) * CHUNKS + i, places, wide[n, rows, lanes], wide[HALO + n, rows, lanes])
            return carry

        lax.fori_loop(0, HALO, plane, 0)

    def inside(x, carry):
        for i in range(CHUNKS):
            lanes = pl.ds(LANES * i, LANES)
            n = (x + HALO) * CHUNKS + i
            put(n, (0, CY + 8), *halo_rows(y_up[x, :, lanes], y_down[x, :, lanes], row))
            for t in range(CY // 8):
                rows = pl.ds(8 * t, 8)
                put(n, (8 * t + 8,), p[x, rows, lanes], k[x, rows, lanes])
        return carry

    def first(x, carry):
        for r in range(6, 74, 8):
            root, sums = around(s, x, x - 1, x + 1, r, lane)
            centre, total = around(q, x, x - 1, x + 1, r, lane)
            for i in range(CHUNKS):
                scaled = conductance * root[i]
                keep = 1.0 - scaled * sums[i]
                a[x * CHUNKS + i, pl.ds(r, 8), :] = keep
                q1[x * CHUNKS + i, pl.ds(r, 8), :] = keep * centre[i] + (scaled * root[i]) * total[i]
        return carry

    def second(x, carry):
        for r in range(7, 73, 8):
            centre, total = around(q1, x, x - 1, x + 1, r, lane)
            for i in range(CHUNKS):
                root = s[x * CHUNKS + i, pl.ds(r, 8), :]
                keep = a[x * CHUNKS + i, pl.ds(r, 8), :]
                q2[x * CHUNKS + i, pl.ds(r, 8), :] = keep * centre[i] + (conductance * root * root) * total[i]
        return carry

    def third(x, carry):
        for r in range(8, 72, 8):
            centre, total = around(q2, x, x - 1, x + 1, r, lane)
            for i in range(CHUNKS):
                root = s[x * CHUNKS + i, pl.ds(r, 8), :]
                keep = a[x * CHUNKS + i, pl.ds(r, 8), :]
                full[x - HALO, pl.ds(r - 8, 8), pl.ds(LANES * i, LANES)] = (
                    keep * centre[i] / root + (conductance * root) * total[i]
                )
        return carry

    outside(x_up, 0)
    outside(x_down, PLANES - HALO)
    begin = 1
    for n in range(4):
        waited(loads[n])
        lax.fori_loop(4 * n, 4 * n + 4, inside, 0)
        end = 4 * n + HALO + 3 if n < 3 else PLANES - 1
        lax.fori_loop(begin, end, first, 0)
        begin = end
    lax.fori_loop(2, PLANES - 2, second, 0)
    stores = []
    for n in range(4):
        lax.fori_loop(HALO + 4 * n, HALO + 4 * n + 4, third, 0)
        planes = pl.ds(4 * n, 4)
        stores += started(pltpu.make_async_copy(full.at[planes], out.at[planes], sems.at[9 + n]))
    waited(ask)

    def answer(d, carry):
        value = jnp.zeros((8, LANES), F32)
        for c in range(3):
            cell = asked[d, c]
            x, y, z = cell >> 15, (cell >> 9) & 63, cell & 511
            lanes = pl.ds(pl.multiple_of((z >> 7) * LANES, LANES), LANES)
            tile = full[x, pl.ds(pl.multiple_of((y >> 3) * 8, 8), 8), lanes]
            tile = pltpu.roll(tile, (LANES + c - (z & 127)) & 127, 1)
            value = jnp.where(jnp.logical_and(row == (y & 7), lane == c), tile, value)
        answers[pl.ds(d, 1), :] = jnp.sum(value, axis=0, keepdims=True)
        return carry

    lax.fori_loop(0, NGX, answer, 0, unroll=4)
    waited(stores)


def diffusion(p, k, y_up, y_down, x_up, x_down, cells):
    return pl.pallas_call(
        diffusion_kernel,
        out_shape=(shape(CX, CY, NZ), shape(NGX, LANES)),
        in_specs=[spec(HBM)] * 2 + [spec()] * 4 + [spec(ANY)],
        out_specs=(spec(HBM), spec()),
        scratch_shapes=[VMEM((PLANES * CHUNKS, ROWS, LANES), F32) for _ in range(5)]
        + [VMEM((CX, CY, NZ), F32) for _ in range(3)]
        + [pltpu.SMEM((NGX, LANES), jnp.int32), DMA((13,))],
        compiler_params=pltpu.CompilerParams(vmem_limit_bytes=34 << 20),
        cost_estimate=pl.CostEstimate(flops=60_000_000, bytes_accessed=12_000_000, transcendentals=0),
        name="diffusion",
    )(far(p), far(k), y_up, y_down, x_up, x_down, cells)


def friction_kernel(rates, answers, terms, state_out, rate_out):
    known = terms[...]
    state, aged, normal, shear, direct, owners, rank = (known[i : i + 1, 0:TRI] for i in range(7))
    got = answers[...]
    named = lax.broadcasted_iota(jnp.int32, (NGX, TRI), 0).astype(F32) == owners
    held = jnp.zeros((NGX, TRI), F32)
    for c in range(3):
        held = jnp.where(jnp.logical_and(named, rank == float(c)), got[:, c : c + 1], held)
    pressure = jnp.sum(held, axis=0, keepdims=True)
    both = jnp.sum(rates[...], axis=0, keepdims=True)
    first, second = both[:, 0:TRI], both[:, TRI : 2 * TRI]
    effective = normal + step_time * second - pressure
    state_out[...] = state
    rate_out[...] = ((shear + step_time * first) / effective - friction_ref - aged) / direct


def friction(*values):
    return pl.pallas_call(
        friction_kernel,
        out_shape=(shape(1, TRI), shape(1, TRI)),
        in_specs=[spec()] * len(values),
        out_specs=(spec(), spec()),
        compiler_params=pltpu.CompilerParams(vmem_limit_bytes=4 << 20),
        name="friction",
    )(*values)


def exchanged(value, axis):
    return lax.all_to_all(value, axis, split_axis=0, concat_axis=0, tiled=True)


def local(
    pressure,
    permeability,
    kernel,
    slip_rate,
    aging_state,
    normal_stress,
    shear_stress,
    direct_effect,
    evolution_effect,
    slip_distance,
    tri_owner,
    tri_cell,
):
    rows = (
        tri_owner,
        tri_cell,
        slip_rate,
        aging_state,
        normal_stress,
        shear_stress,
        direct_effect,
        evolution_effect,
        slip_distance,
    )
    y_up, y_down = pack(pressure, permeability)
    wanted, terms = prepare(*[v.reshape(1, TRI) for v in rows])
    y_up, y_down = lax.ppermute(y_up, "gy", Y_UP), lax.ppermute(y_down, "gy", Y_DOWN)
    lane = lax.broadcasted_iota(jnp.int32, (NGX, LANES), 1)
    row = jnp.pad(lax.ppermute(slip_rate, ("gx", "gy"), SLIP_MOVES), (0, LANES - TRI)).reshape(1, LANES)
    leaving = jnp.where(lane < TRI, row, wanted)
    arrived = exchanged(leaving, "gx")
    x_up, x_down = sides(pressure, permeability, y_up, y_down, leaving)
    x_up, x_down = lax.ppermute(x_up, "gx", X_UP), lax.ppermute(x_down, "gx", X_DOWN)
    partial_sums, cells = partial_rates(arrived, kernel)
    rates = exchanged(partial_sums, "gy")
    field, answers = diffusion(pressure, permeability, y_up, y_down, x_up, x_down, cells)
    answers = exchanged(answers, "gx")
    state_next, log_rate = friction(rates, answers, terms)
    return field, state_next.reshape(TRI), log_rate.reshape(TRI)


def solution(mesh):
    both = P(("gx", "gy"))
    placed = (
        P("gx", "gy", None),
        P("gx", "gy", None),
        P(None, "gx", "gy"),
        *([both] * 7),
        P(("gx", "gy"), None),
        both,
    )
    return jax.shard_map(
        local,
        mesh=mesh,
        in_specs=placed,
        out_specs=(P("gx", "gy", None), both, both),
        check_vma=False,
    )
```

```python
import jax
import jax.numpy as jnp
from jax import lax
from jax.experimental import pallas as pl
from jax.experimental.pallas import tpu as pltpu
from jax.sharding import PartitionSpec as P

NGX, NGY = 32, 8
CX, CY, NZ, TRI = 16, 64, 512, 48
HALO = 3
ROWS = 80
LANES = 128
CHUNKS = NZ // LANES
conductance = 0.15
step_time = 1.0
heal_time = 0.5
friction_ref = 0.6
F32 = jnp.float32
VMEM = pltpu.VMEM
ANY = pl.ANY

X_MOVE = (2, 1, 2, 1, 0, 3, 0, 3)
Y_MOVE = (1, 1, 0, 0, 0, 0, 1, 1)
X_CODE = sum(v << (2 * i) for i, v in enumerate(X_MOVE))
Y_CODE = sum(v << i for i, v in enumerate(Y_MOVE))


def landing(group, other):
    delta = (other - group) & 7
    x = ((group >> 1) + ((X_CODE >> (2 * delta)) & 3)) & 3
    y = (group & 1) ^ ((Y_CODE >> delta) & 1)
    return 2 * x + y


SLIP_MOVES = [
    ((4 * g + r) * NGY + j, (4 * landing(g, j) + r) * NGY + g) for g in range(8) for r in range(4) for j in range(NGY)
]
X_UP = [(i, i + 1) for i in range(NGX - 1)]
X_DOWN = [(j, i) for i, j in X_UP]
Y_UP = [(i, i + 1) for i in range(NGY - 1)]
Y_DOWN = [(j, i) for i, j in Y_UP]


def spec(space=VMEM):
    return pl.BlockSpec(memory_space=space)


def shape(*dims, dtype=F32):
    return jax.ShapeDtypeStruct(dims, dtype)


def far(value):
    return pltpu.with_memory_space_constraint(value, pltpu.HBM)


def all_far(*values):
    return tuple(far(v) for v in values)


def started(*copies):
    for copy in copies:
        copy.start()
    return copies


def waited(copies):
    for copy in copies:
        copy.wait()


HBM = pltpu.HBM
DMA = pltpu.SemaphoreType.DMA


def turned(row_value):
    row = lax.broadcasted_iota(jnp.int32, (TRI, TRI), 0)
    column = lax.broadcasted_iota(jnp.int32, (TRI, TRI), 1)
    return jnp.sum(jnp.where(row == column, row_value, 0.0), axis=1, keepdims=True)


def pack_kernel(p, k, y_up, y_down, x_up, x_down, tiles, sems):
    tops = started(
        pltpu.make_async_copy(p.at[:, pl.ds(CY - 8, 8), :], tiles.at[0], sems.at[0]),
        pltpu.make_async_copy(k.at[:, pl.ds(CY - 8, 8), :], tiles.at[1], sems.at[1]),
        pltpu.make_async_copy(p.at[:, pl.ds(0, 8), :], tiles.at[2], sems.at[2]),
        pltpu.make_async_copy(k.at[:, pl.ds(0, 8), :], tiles.at[3], sems.at[3]),
    )
    copies = []
    for side, (target, start) in enumerate(((x_up, CX - HALO), (x_down, 0))):
        for n, source in enumerate((p, k)):
            copies.append(
                pltpu.make_async_copy(
                    source.at[pl.ds(start, HALO)],
                    target.at[pl.ds(HALO * n, HALO), pl.ds(0, CY)],
                    sems.at[4 + 2 * side + n],
                )
            )
    started(*copies)
    row = lax.broadcasted_iota(jnp.int32, (8, NZ), 0)
    waited(tops)

    def plane(x, carry):
        y_up[x] = jnp.where(row >= 5, tiles[0, x], pltpu.roll(tiles[1, x], 3, 0))
        y_down[x] = jnp.where(row < 3, tiles[2, x], pltpu.roll(tiles[3, x], 5, 0))
        return carry

    lax.fori_loop(0, CX, plane, 0)
    waited(copies)


def pack(p, k):
    return pl.pallas_call(
        pack_kernel,
        out_shape=(shape(CX, 8, NZ),) * 2 + (HBM((2 * HALO, CY + 8, NZ), F32),) * 2,
        in_specs=[spec(HBM)] * 2,
        out_specs=(spec(),) * 2 + (spec(HBM),) * 2,
        scratch_shapes=[VMEM((4, CX, 8, NZ), F32), DMA((8,))],
        compiler_params=pltpu.CompilerParams(vmem_limit_bytes=4 << 20),
        name="pack",
    )(far(p), far(k))


def prepare_kernel(owner, cell, *refs):
    floats, (wanted, terms, whole, held, sems) = refs[:7], refs[7:]
    waited(
        started(
            pltpu.make_async_copy(owner, whole.at[0], sems.at[0]),
            pltpu.make_async_copy(cell, whole.at[1], sems.at[1]),
            *[pltpu.make_async_copy(ref, held.at[n], sems.at[2 + n]) for n, ref in enumerate(floats)],
        )
    )
    slip, aging, normal, shear, direct, evolution, distance = (held[n] for n in range(7))
    owners = whole[0].astype(F32)
    first = lax.broadcasted_iota(jnp.int32, (TRI, TRI), 0)
    second = lax.broadcasted_iota(jnp.int32, (TRI, TRI), 1)
    same = jnp.logical_and(turned(owners) == owners, first < second)
    rank = jnp.sum(jnp.where(same, 1.0, 0.0), axis=0, keepdims=True)
    cells = whole[1].astype(F32)
    lane = lax.broadcasted_iota(jnp.int32, (NGX, LANES), 1)
    named = lax.broadcasted_iota(jnp.int32, (NGX, TRI), 0) == whole[0]
    value = jnp.zeros((NGX, LANES), F32)
    for c in range(3):
        asked = jnp.where(jnp.logical_and(named, rank == float(c)), cells, 0.0)
        value = jnp.where(lane == TRI + c, jnp.sum(asked, axis=1, keepdims=True), value)
    wanted[...] = value
    ratio = distance / slip
    state = ratio + (aging - ratio) * jnp.exp(-heal_time / ratio)
    terms[...] = jnp.zeros((8, LANES), F32)
    aged = evolution * jnp.log(state / distance)
    for n, term in enumerate((state, aged, normal, shear, direct, owners, rank)):
        terms[n : n + 1, 0:TRI] = term


def prepare(*values):
    return pl.pallas_call(
        prepare_kernel,
        out_shape=(shape(NGX, LANES), shape(8, LANES)),
        in_specs=[spec(HBM)] * len(values),
        out_specs=(spec(),) * 2,
        scratch_shapes=[VMEM((2, 1, TRI), jnp.int32), VMEM((7, 1, TRI), F32), DMA((9,))],
        compiler_params=pltpu.CompilerParams(vmem_limit_bytes=2 << 20),
        name="prepare",
    )(*all_far(*values))


def halo_rows(low, high, row):
    p = jnp.where(row >= 5, low, jnp.where(row < 3, high, 0.0))
    k = jnp.where(row >= 5, pltpu.roll(low, 5, 0), jnp.where(row < 3, pltpu.roll(high, 3, 0), 0.0))
    return p, k


def sides_kernel(x_up, x_down, y_up, y_down, token, x_up_out, x_down_out, tiles, sems):
    del x_up, x_down, token
    row = lax.broadcasted_iota(jnp.int32, (8, NZ), 0)
    copies = []
    for side, (target, start) in enumerate(((x_up_out, CX - HALO), (x_down_out, 0))):
        for n in range(HALO):
            tiles[side, n], tiles[side, HALO + n] = halo_rows(y_up[start + n], y_down[start + n], row)
        copies += started(pltpu.make_async_copy(tiles.at[side], target.at[:, pl.ds(CY, 8)], sems.at[side]))
    waited(copies)


def sides(x_up, x_down, y_up, y_down, token):
    return pl.pallas_call(
        sides_kernel,
        out_shape=(HBM((2 * HALO, CY + 8, NZ), F32),) * 2,
        in_specs=[spec(HBM)] * 2 + [spec()] * 2 + [spec(ANY)],
        out_specs=(spec(HBM),) * 2,
        scratch_shapes=[VMEM((2, 2 * HALO, 8, NZ), F32), DMA((2,))],
        input_output_aliases={0: 0, 1: 1},
        compiler_params=pltpu.CompilerParams(vmem_limit_bytes=4 << 20),
        name="sides",
    )(far(x_up), far(x_down), y_up, y_down, token)


def rates_kernel(arrived, kernel_far, out, cells, acc, kernel, sems):
    copies = started(
        *[
            pltpu.make_async_copy(
                kernel_far.at[n // 4, pl.ds(96 * (n % 4), 96)], kernel.at[n // 4, pl.ds(96 * (n % 4), 96)], sems.at[n]
            )
            for n in range(8)
        ]
    )
    gy = lax.axis_index("gy")
    lane = lax.broadcasted_iota(jnp.int32, (1, LANES), 1)
    chunks = [jnp.zeros((1, LANES), F32) for _ in range(12)]
    for j in range(NGY):
        spot = landing(gy, j)
        for r in range(4):
            start = (r * NGY + j) * TRI
            chunk, offset = divmod(start, LANES)
            row = pltpu.roll(arrived[pl.ds(4 * spot + r, 1), :], offset, 1)
            inside = jnp.logical_and(lane >= offset, lane < offset + TRI)
            chunks[chunk] = jnp.where(inside, row, chunks[chunk])
            if offset + TRI > LANES:
                chunks[chunk + 1] = jnp.where(lane < offset + TRI - LANES, row, chunks[chunk + 1])
    cells[...] = pltpu.roll(arrived[...], LANES - TRI, 1).astype(jnp.int32)
    wide = [jnp.broadcast_to(c, (8, LANES)) for c in chunks]

    for n in range(8):
        part = n // 4
        copies[n].wait()

        def tile(t, carry):
            rows = pl.ds(pl.multiple_of(t * 8, 8), 8)
            terms = [kernel[part, rows, pl.ds(LANES * c, LANES)] * wide[c] for c in range(12)]
            while len(terms) > 1:
                terms = [a + b for a, b in zip(terms[::2], terms[1::2])] + terms[len(terms) // 2 * 2 :]
            dest = (t // 6) * 96 + part * TRI + (t % 6) * 8
            acc[pl.ds(pl.multiple_of(dest, 8), 8), :] = terms[0]
            return carry

        lax.fori_loop(12 * (n % 4), 12 * (n % 4) + 12, tile, 0, unroll=4)
    row8 = lax.broadcasted_iota(jnp.int32, (8, LANES), 0)
    total = jnp.zeros((8, 2 * TRI), F32)
    for j in range(NGY):
        total = total + lax.dot_general(
            jnp.where(row8 == j, 1.0, 0.0),
            acc[pl.ds(2 * TRI * j, 2 * TRI), :],
            (((1,), (1,)), ((), ())),
            precision=lax.Precision.HIGHEST,
            preferred_element_type=F32,
        )
    out[...] = jnp.zeros((8, LANES), F32)
    out[:, 0 : 2 * TRI] = total


def partial_rates(arrived, kernel):
    return pl.pallas_call(
        rates_kernel,
        out_shape=(shape(NGY, LANES), shape(NGX, LANES, dtype=jnp.int32)),
        in_specs=[spec(), spec(HBM)],
        out_specs=(spec(), spec()),
        scratch_shapes=[VMEM((768, LANES), F32), VMEM(kernel.shape, F32), DMA((8,))],
        compiler_params=pltpu.CompilerParams(vmem_limit_bytes=8 << 20),
        cost_estimate=pl.CostEstimate(flops=1000000000000, bytes_accessed=6000000000, transcendentals=0),
        name="rates",
    )(arrived, far(kernel))


def around(ref, x, before, after, row, lane):
    rows = pl.ds(row, 8)
    centre = [ref[x * CHUNKS + i, rows, :] for i in range(CHUNKS)]
    left = [pltpu.roll(v, 1, 1) for v in centre]
    right = [pltpu.roll(v, LANES - 1, 1) for v in centre]
    sums = []
    for i in range(CHUNKS):
        below = left[i - 1] if i else 0.0
        above = right[i + 1] if i + 1 < CHUNKS else 0.0
        z = jnp.where(lane == 0, below, left[i]) + jnp.where(lane == LANES - 1, above, right[i])
        y = ref[x * CHUNKS + i, pl.ds(row - 1, 8), :] + ref[x * CHUNKS + i, pl.ds(row + 1, 8), :]
        xs = ref[before * CHUNKS + i, rows, :] + ref[after * CHUNKS + i, rows, :]
        sums.append((xs + y) + z)
    return centre, sums


PLANES = CX + 2 * HALO


def diffusion_kernel(
    p_far, k_far, y_up, y_down, x_up, x_down, cells, out, answers, s, q, a, q1, q2, p, k, full, wide, asked, sems
):
    loads = []
    low = started(pltpu.make_async_copy(x_up, wide.at[0], sems.at[12]))
    for n in range(4):
        planes = pl.ds(4 * n, 4)
        loads.append(
            started(
                pltpu.make_async_copy(p_far.at[planes], p.at[planes], sems.at[2 * n]),
                pltpu.make_async_copy(k_far.at[planes], k.at[planes], sems.at[2 * n + 1]),
            )
        )
    high = started(pltpu.make_async_copy(x_down, wide.at[1], sems.at[13]))
    ask = started(pltpu.make_async_copy(cells, asked, sems.at[8]))
    lane = lax.broadcasted_iota(jnp.int32, (8, LANES), 1)
    row = lax.broadcasted_iota(jnp.int32, (8, LANES), 0)

    def put(n, places, p_tile, k_tile):
        root = jnp.sqrt(k_tile)
        scaled = root * p_tile
        for place in places:
            s[n, place : place + 8, :] = root
            q[n, place : place + 8, :] = scaled

    def outside(side, base):
        def plane(n, carry):
            for i in range(CHUNKS):
                lanes = pl.ds(LANES * i, LANES)
                for t in range(CY // 8 + 1):
                    places = (8 * t + 8,) if t < CY // 8 else (0, CY + 8)
                    rows = pl.ds(8 * t, 8)
                    put((base + n) * CHUNKS + i, places, wide[side, n, rows, lanes], wide[side, HALO + n, rows, lanes])
            return carry

        lax.fori_loop(0, HALO, plane, 0)

    def inside(x, carry):
        for i in range(CHUNKS):
            lanes = pl.ds(LANES * i, LANES)
            n = (x + HALO) * CHUNKS + i
            put(n, (0, CY + 8), *halo_rows(y_up[x, :, lanes], y_down[x, :, lanes], row))
            for t in range(CY // 8):
                rows = pl.ds(8 * t, 8)
                put(n, (8 * t + 8,), p[x, rows, lanes], k[x, rows, lanes])
        return carry

    def first(x, carry):
        for r in range(6, 74, 8):
            root, sums = around(s, x, x - 1, x + 1, r, lane)
            centre, total = around(q, x, x - 1, x + 1, r, lane)
            for i in range(CHUNKS):
                scaled = conductance * root[i]
                keep = 1.0 - scaled * sums[i]
                a[x * CHUNKS + i, pl.ds(r, 8), :] = keep
                q1[x * CHUNKS + i, pl.ds(r, 8), :] = keep * centre[i] + (scaled * root[i]) * total[i]
        return carry

    def second(x, carry):
        for r in range(7, 73, 8):
            centre, total = around(q1, x, x - 1, x + 1, r, lane)
            for i in range(CHUNKS):
                root = s[x * CHUNKS + i, pl.ds(r, 8), :]
                keep = a[x * CHUNKS + i, pl.ds(r, 8), :]
                q2[x * CHUNKS + i, pl.ds(r, 8), :] = keep * centre[i] + (conductance * root * root) * total[i]
        return carry

    def third(x, carry):
        for r in range(8, 72, 8):
            centre, total = around(q2, x, x - 1, x + 1, r, lane)
            for i in range(CHUNKS):
                root = s[x * CHUNKS + i, pl.ds(r, 8), :]
                keep = a[x * CHUNKS + i, pl.ds(r, 8), :]
                full[x - HALO, pl.ds(r - 8, 8), pl.ds(LANES * i, LANES)] = (
                    keep * centre[i] / root + (conductance * root) * total[i]
                )
        return carry

    waited(low)
    outside(0, 0)

    def run(begin, end, *stages):
        def step(x, carry):
            for stage, shift in stages:
                stage(x + shift, 0)
            return carry

        lax.fori_loop(begin, end, step, 0)

    t, u, f, c = (third, -3), (second, -1), (first, 1), (inside, 0)
    stores = []
    waited(loads[0])
    run(0, 3, f, c)
    run(3, 4, u, f, c)
    waited(loads[1])
    run(4, 6, u, f, c)
    run(6, 8, t, u, f, c)
    waited(loads[2] + loads[3])
    run(8, 14, t, u, f, c)
    stores += started(pltpu.make_async_copy(full.at[pl.ds(0, 8)], out.at[pl.ds(0, 8)], sems.at[9]))
    run(14, 16, t, u, f, c)
    waited(high)
    outside(1, PLANES - HALO)
    run(16, 20, t, u, f)
    stores += started(pltpu.make_async_copy(full.at[pl.ds(8, 6)], out.at[pl.ds(8, 6)], sems.at[10]))
    run(20, 21, t, u)
    run(21, 22, t)
    stores += started(pltpu.make_async_copy(full.at[pl.ds(14, 2)], out.at[pl.ds(14, 2)], sems.at[11]))
    waited(ask)

    def answer(d, carry):
        value = jnp.zeros((8, LANES), F32)
        for c in range(3):
            cell = asked[d, c]
            x, y, z = cell >> 15, (cell >> 9) & 63, cell & 511
            lanes = pl.ds(pl.multiple_of((z >> 7) * LANES, LANES), LANES)
            tile = full[x, pl.ds(pl.multiple_of((y >> 3) * 8, 8), 8), lanes]
            tile = pltpu.roll(tile, (LANES + c - (z & 127)) & 127, 1)
            value = jnp.where(jnp.logical_and(row == (y & 7), lane == c), tile, value)
        answers[pl.ds(d, 1), :] = jnp.sum(value, axis=0, keepdims=True)
        return carry

    lax.fori_loop(0, NGX, answer, 0, unroll=4)
    waited(stores)


def diffusion(p, k, y_up, y_down, x_up, x_down, cells):
    return pl.pallas_call(
        diffusion_kernel,
        out_shape=(shape(CX, CY, NZ), shape(NGX, LANES)),
        in_specs=[spec(HBM)] * 2 + [spec()] * 2 + [spec(ANY)] * 3,
        out_specs=(spec(HBM), spec()),
        scratch_shapes=[VMEM((PLANES * CHUNKS, ROWS, LANES), F32) for _ in range(5)]
        + [VMEM((CX, CY, NZ), F32) for _ in range(3)]
        + [VMEM((2, 2 * HALO, CY + 8, NZ), F32), pltpu.SMEM((NGX, LANES), jnp.int32), DMA((14,))],
        compiler_params=pltpu.CompilerParams(vmem_limit_bytes=34 << 20),
        cost_estimate=pl.CostEstimate(flops=60_000_000, bytes_accessed=12_000_000, transcendentals=0),
        name="diffusion",
    )(far(p), far(k), y_up, y_down, x_up, x_down, cells)


def friction_kernel(rates, answers, terms, state_out, rate_out):
    known = terms[...]
    state, aged, normal, shear, direct, owners, rank = (known[i : i + 1, 0:TRI] for i in range(7))
    got = answers[...]
    named = lax.broadcasted_iota(jnp.int32, (NGX, TRI), 0).astype(F32) == owners
    held = jnp.zeros((NGX, TRI), F32)
    for c in range(3):
        held = jnp.where(jnp.logical_and(named, rank == float(c)), got[:, c : c + 1], held)
    pressure = jnp.sum(held, axis=0, keepdims=True)
    both = jnp.sum(rates[...], axis=0, keepdims=True)
    first, second = both[:, 0:TRI], both[:, TRI : 2 * TRI]
    effective = normal + step_time * second - pressure
    state_out[...] = state
    rate_out[...] = ((shear + step_time * first) / effective - friction_ref - aged) / direct


def friction(*values):
    return pl.pallas_call(
        friction_kernel,
        out_shape=(shape(1, TRI), shape(1, TRI)),
        in_specs=[spec()] * len(values),
        out_specs=(spec(), spec()),
        compiler_params=pltpu.CompilerParams(vmem_limit_bytes=4 << 20),
        name="friction",
    )(*values)


def exchanged(value, axis):
    return lax.all_to_all(value, axis, split_axis=0, concat_axis=0, tiled=True)


def local(
    pressure,
    permeability,
    kernel,
    slip_rate,
    aging_state,
    normal_stress,
    shear_stress,
    direct_effect,
    evolution_effect,
    slip_distance,
    tri_owner,
    tri_cell,
):
    rows = (
        tri_owner,
        tri_cell,
        slip_rate,
        aging_state,
        normal_stress,
        shear_stress,
        direct_effect,
        evolution_effect,
        slip_distance,
    )
    y_up, y_down, x_up, x_down = pack(pressure, permeability)
    wanted, terms = prepare(*[v.reshape(1, TRI) for v in rows])
    y_up, y_down = lax.ppermute(y_up, "gy", Y_UP), lax.ppermute(y_down, "gy", Y_DOWN)
    lane = lax.broadcasted_iota(jnp.int32, (NGX, LANES), 1)
    row = jnp.pad(lax.ppermute(slip_rate, ("gx", "gy"), SLIP_MOVES), (0, LANES - TRI)).reshape(1, LANES)
    leaving = jnp.where(lane < TRI, row, wanted)
    arrived = exchanged(leaving, "gx")
    x_up, x_down = sides(x_up, x_down, y_up, y_down, leaving)
    x_up, x_down = lax.ppermute(x_up, "gx", X_UP), lax.ppermute(x_down, "gx", X_DOWN)
    partial_sums, cells = partial_rates(arrived, kernel)
    rates = exchanged(partial_sums, "gy")
    field, answers = diffusion(pressure, permeability, y_up, y_down, x_up, x_down, cells)
    answers = exchanged(answers, "gx")
    state_next, log_rate = friction(rates, answers, terms)
    return field, state_next.reshape(TRI), log_rate.reshape(TRI)


def solution(mesh):
    both = P(("gx", "gy"))
    placed = (
        P("gx", "gy", None),
        P("gx", "gy", None),
        P(None, "gx", "gy"),
        *([both] * 7),
        P(("gx", "gy"), None),
        both,
    )
    return jax.shard_map(
        local,
        mesh=mesh,
        in_specs=placed,
        out_specs=(P("gx", "gy", None), both, both),
        check_vma=False,
    )
```

```python
import jax
import jax.numpy as jnp
from jax import lax
from jax.experimental import pallas as pl
from jax.experimental.pallas import tpu as pltpu
from jax.sharding import PartitionSpec as P

NGX, NGY = 32, 8
CX, CY, NZ, TRI = 16, 64, 512, 48
HALO = 3
ROWS = 80
LANES = 128
CHUNKS = NZ // LANES
conductance = 0.15
step_time = 1.0
heal_time = 0.5
friction_ref = 0.6
F32 = jnp.float32
VMEM = pltpu.VMEM
ANY = pl.ANY

X_MOVE = (2, 1, 2, 1, 0, 3, 0, 3)
Y_MOVE = (1, 1, 0, 0, 0, 0, 1, 1)
X_CODE = sum(v << (2 * i) for i, v in enumerate(X_MOVE))
Y_CODE = sum(v << i for i, v in enumerate(Y_MOVE))


def landing(group, other):
    delta = (other - group) & 7
    x = ((group >> 1) + ((X_CODE >> (2 * delta)) & 3)) & 3
    y = (group & 1) ^ ((Y_CODE >> delta) & 1)
    return 2 * x + y


SLIP_MOVES = [
    ((4 * g + r) * NGY + j, (4 * landing(g, j) + r) * NGY + g) for g in range(8) for r in range(4) for j in range(NGY)
]
X_UP = [(i, i + 1) for i in range(NGX - 1)]
X_DOWN = [(j, i) for i, j in X_UP]
Y_UP = [(i, i + 1) for i in range(NGY - 1)]
Y_DOWN = [(j, i) for i, j in Y_UP]


def spec(space=VMEM):
    return pl.BlockSpec(memory_space=space)


def shape(*dims, dtype=F32):
    return jax.ShapeDtypeStruct(dims, dtype)


def far(value):
    return pltpu.with_memory_space_constraint(value, pltpu.HBM)


def all_far(*values):
    return tuple(far(v) for v in values)


def started(*copies):
    for copy in copies:
        copy.start()
    return copies


def waited(copies):
    for copy in copies:
        copy.wait()


HBM = pltpu.HBM
DMA = pltpu.SemaphoreType.DMA


def turned(row_value):
    row = lax.broadcasted_iota(jnp.int32, (TRI, TRI), 0)
    column = lax.broadcasted_iota(jnp.int32, (TRI, TRI), 1)
    return jnp.sum(jnp.where(row == column, row_value, 0.0), axis=1, keepdims=True)


def pack_kernel(p, k, y_up, y_down, x_up, x_down, tiles, rows, sems):
    tops = started(
        pltpu.make_async_copy(p.at[:, pl.ds(CY - 8, 8), :], tiles.at[0], sems.at[0]),
        pltpu.make_async_copy(k.at[:, pl.ds(CY - 8, 8), :], tiles.at[1], sems.at[1]),
        pltpu.make_async_copy(p.at[:, pl.ds(0, 8), :], tiles.at[2], sems.at[2]),
        pltpu.make_async_copy(k.at[:, pl.ds(0, 8), :], tiles.at[3], sems.at[3]),
    )
    loads = [
        started(
            *[
                pltpu.make_async_copy(
                    source.at[pl.ds(start, HALO)], rows.at[side, pl.ds(HALO * n, HALO)], sems.at[4 + 2 * side + n]
                )
                for n, source in enumerate((p, k))
            ]
        )
        for side, start in enumerate((CX - HALO, 0))
    ]
    row = lax.broadcasted_iota(jnp.int32, (8, NZ), 0)
    waited(tops)

    def plane(x, carry):
        y_up[x] = jnp.where(row >= 5, tiles[0, x], pltpu.roll(tiles[1, x], 3, 0))
        y_down[x] = jnp.where(row < 3, tiles[2, x], pltpu.roll(tiles[3, x], 5, 0))
        return carry

    lax.fori_loop(0, CX, plane, 0)
    stores = []
    for side, target in enumerate((x_up, x_down)):
        waited(loads[side])
        stores += started(pltpu.make_async_copy(rows.at[side], target.at[:, pl.ds(0, CY)], sems.at[8 + side]))
    waited(stores)


def pack(p, k):
    return pl.pallas_call(
        pack_kernel,
        out_shape=(shape(CX, 8, NZ),) * 2 + (HBM((2 * HALO, CY + 8, NZ), F32),) * 2,
        in_specs=[spec(HBM)] * 2,
        out_specs=(spec(),) * 2 + (spec(HBM),) * 2,
        scratch_shapes=[VMEM((4, CX, 8, NZ), F32), VMEM((2, 2 * HALO, CY, NZ), F32), DMA((10,))],
        compiler_params=pltpu.CompilerParams(vmem_limit_bytes=6 << 20),
        name="pack",
    )(far(p), far(k))


def prepare_kernel(owner, cell, *refs):
    floats, (wanted, terms, whole, held, sems) = refs[:7], refs[7:]
    waited(
        started(
            pltpu.make_async_copy(owner, whole.at[0], sems.at[0]),
            pltpu.make_async_copy(cell, whole.at[1], sems.at[1]),
            *[pltpu.make_async_copy(ref, held.at[n], sems.at[2 + n]) for n, ref in enumerate(floats)],
        )
    )
    slip, aging, normal, shear, direct, evolution, distance = (held[n] for n in range(7))
    owners = whole[0].astype(F32)
    first = lax.broadcasted_iota(jnp.int32, (TRI, TRI), 0)
    second = lax.broadcasted_iota(jnp.int32, (TRI, TRI), 1)
    same = jnp.logical_and(turned(owners) == owners, first < second)
    rank = jnp.sum(jnp.where(same, 1.0, 0.0), axis=0, keepdims=True)
    cells = whole[1].astype(F32)
    lane = lax.broadcasted_iota(jnp.int32, (NGX, LANES), 1)
    named = lax.broadcasted_iota(jnp.int32, (NGX, TRI), 0) == whole[0]
    value = jnp.zeros((NGX, LANES), F32)
    for c in range(3):
        asked = jnp.where(jnp.logical_and(named, rank == float(c)), cells, 0.0)
        value = jnp.where(lane == TRI + c, jnp.sum(asked, axis=1, keepdims=True), value)
    wanted[...] = value
    ratio = distance / slip
    state = ratio + (aging - ratio) * jnp.exp(-heal_time / ratio)
    terms[...] = jnp.zeros((8, LANES), F32)
    aged = evolution * jnp.log(state / distance)
    for n, term in enumerate((state, aged, normal, shear, direct, owners, rank)):
        terms[n : n + 1, 0:TRI] = term


def prepare(*values):
    return pl.pallas_call(
        prepare_kernel,
        out_shape=(shape(NGX, LANES), shape(8, LANES)),
        in_specs=[spec(HBM)] * len(values),
        out_specs=(spec(),) * 2,
        scratch_shapes=[VMEM((2, 1, TRI), jnp.int32), VMEM((7, 1, TRI), F32), DMA((9,))],
        compiler_params=pltpu.CompilerParams(vmem_limit_bytes=2 << 20),
        name="prepare",
    )(*all_far(*values))


def halo_rows(low, high, row):
    p = jnp.where(row >= 5, low, jnp.where(row < 3, high, 0.0))
    k = jnp.where(row >= 5, pltpu.roll(low, 5, 0), jnp.where(row < 3, pltpu.roll(high, 3, 0), 0.0))
    return p, k


def sides_kernel(x_up, x_down, y_up, y_down, token, x_up_out, x_down_out, tiles, sems):
    del x_up, x_down, token
    row = lax.broadcasted_iota(jnp.int32, (8, NZ), 0)
    copies = []
    for side, (target, start) in enumerate(((x_up_out, CX - HALO), (x_down_out, 0))):
        for n in range(HALO):
            tiles[side, n], tiles[side, HALO + n] = halo_rows(y_up[start + n], y_down[start + n], row)
        copies += started(pltpu.make_async_copy(tiles.at[side], target.at[:, pl.ds(CY, 8)], sems.at[side]))
    waited(copies)


def sides(x_up, x_down, y_up, y_down, token):
    return pl.pallas_call(
        sides_kernel,
        out_shape=(HBM((2 * HALO, CY + 8, NZ), F32),) * 2,
        in_specs=[spec(HBM)] * 2 + [spec()] * 2 + [spec(ANY)],
        out_specs=(spec(HBM),) * 2,
        scratch_shapes=[VMEM((2, 2 * HALO, 8, NZ), F32), DMA((2,))],
        input_output_aliases={0: 0, 1: 1},
        compiler_params=pltpu.CompilerParams(vmem_limit_bytes=4 << 20),
        name="sides",
    )(far(x_up), far(x_down), y_up, y_down, token)


def rates_kernel(arrived, kernel_far, out, cells, acc, kernel, sems):
    copies = started(
        *[
            pltpu.make_async_copy(
                kernel_far.at[n // 4, pl.ds(96 * (n % 4), 96)], kernel.at[n // 4, pl.ds(96 * (n % 4), 96)], sems.at[n]
            )
            for n in range(8)
        ]
    )
    gy = lax.axis_index("gy")
    lane = lax.broadcasted_iota(jnp.int32, (1, LANES), 1)
    chunks = [jnp.zeros((1, LANES), F32) for _ in range(12)]
    for j in range(NGY):
        spot = landing(gy, j)
        for r in range(4):
            start = (r * NGY + j) * TRI
            chunk, offset = divmod(start, LANES)
            row = pltpu.roll(arrived[pl.ds(4 * spot + r, 1), :], offset, 1)
            inside = jnp.logical_and(lane >= offset, lane < offset + TRI)
            chunks[chunk] = jnp.where(inside, row, chunks[chunk])
            if offset + TRI > LANES:
                chunks[chunk + 1] = jnp.where(lane < offset + TRI - LANES, row, chunks[chunk + 1])
    cells[...] = pltpu.roll(arrived[...], LANES - TRI, 1).astype(jnp.int32)
    wide = [jnp.broadcast_to(c, (8, LANES)) for c in chunks]

    for n in range(8):
        part = n // 4
        copies[n].wait()

        def tile(t, carry):
            rows = pl.ds(pl.multiple_of(t * 8, 8), 8)
            terms = [kernel[part, rows, pl.ds(LANES * c, LANES)] * wide[c] for c in range(12)]
            while len(terms) > 1:
                terms = [a + b for a, b in zip(terms[::2], terms[1::2])] + terms[len(terms) // 2 * 2 :]
            dest = (t // 6) * 96 + part * TRI + (t % 6) * 8
            acc[pl.ds(pl.multiple_of(dest, 8), 8), :] = terms[0]
            return carry

        lax.fori_loop(12 * (n % 4), 12 * (n % 4) + 12, tile, 0, unroll=4)
    row8 = lax.broadcasted_iota(jnp.int32, (8, LANES), 0)
    total = jnp.zeros((8, 2 * TRI), F32)
    for j in range(NGY):
        total = total + lax.dot_general(
            jnp.where(row8 == j, 1.0, 0.0),
            acc[pl.ds(2 * TRI * j, 2 * TRI), :],
            (((1,), (1,)), ((), ())),
            precision=lax.Precision.HIGHEST,
            preferred_element_type=F32,
        )
    out[...] = jnp.zeros((8, LANES), F32)
    out[:, 0 : 2 * TRI] = total


def partial_rates(arrived, kernel):
    return pl.pallas_call(
        rates_kernel,
        out_shape=(shape(NGY, LANES), shape(NGX, LANES, dtype=jnp.int32)),
        in_specs=[spec(), spec(HBM)],
        out_specs=(spec(), spec()),
        scratch_shapes=[VMEM((768, LANES), F32), VMEM(kernel.shape, F32), DMA((8,))],
        compiler_params=pltpu.CompilerParams(vmem_limit_bytes=8 << 20),
        cost_estimate=pl.CostEstimate(flops=1000000000000, bytes_accessed=6000000000, transcendentals=0),
        name="rates",
    )(arrived, far(kernel))


def around(ref, x, before, after, row, lane):
    rows = pl.ds(row, 8)
    centre = [ref[x * CHUNKS + i, rows, :] for i in range(CHUNKS)]
    left = [pltpu.roll(v, 1, 1) for v in centre]
    right = [pltpu.roll(v, LANES - 1, 1) for v in centre]
    sums = []
    for i in range(CHUNKS):
        below = left[i - 1] if i else 0.0
        above = right[i + 1] if i + 1 < CHUNKS else 0.0
        z = jnp.where(lane == 0, below, left[i]) + jnp.where(lane == LANES - 1, above, right[i])
        y = ref[x * CHUNKS + i, pl.ds(row - 1, 8), :] + ref[x * CHUNKS + i, pl.ds(row + 1, 8), :]
        xs = ref[before * CHUNKS + i, rows, :] + ref[after * CHUNKS + i, rows, :]
        sums.append((xs + y) + z)
    return centre, sums


PLANES = CX + 2 * HALO


def diffusion_kernel(
    p_far, k_far, y_up, y_down, x_up, x_down, cells, out, answers, s, q, a, q1, q2, p, k, full, wide, asked, sems
):
    loads = []
    low = started(pltpu.make_async_copy(x_up, wide.at[0], sems.at[12]))
    for n in range(4):
        planes = pl.ds(4 * n, 4)
        loads.append(
            started(
                pltpu.make_async_copy(p_far.at[planes], p.at[planes], sems.at[2 * n]),
                pltpu.make_async_copy(k_far.at[planes], k.at[planes], sems.at[2 * n + 1]),
            )
        )
    high = started(pltpu.make_async_copy(x_down, wide.at[1], sems.at[13]))
    ask = started(pltpu.make_async_copy(cells, asked, sems.at[8]))
    lane = lax.broadcasted_iota(jnp.int32, (8, LANES), 1)
    row = lax.broadcasted_iota(jnp.int32, (8, LANES), 0)

    def put(n, places, p_tile, k_tile):
        root = jnp.sqrt(k_tile)
        scaled = root * p_tile
        for place in places:
            s[n, place : place + 8, :] = root
            q[n, place : place + 8, :] = scaled

    def outside(side, base):
        def plane(n, carry):
            for i in range(CHUNKS):
                lanes = pl.ds(LANES * i, LANES)
                for t in range(CY // 8 + 1):
                    places = (8 * t + 8,) if t < CY // 8 else (0, CY + 8)
                    rows = pl.ds(8 * t, 8)
                    put((base + n) * CHUNKS + i, places, wide[side, n, rows, lanes], wide[side, HALO + n, rows, lanes])
            return carry

        lax.fori_loop(0, HALO, plane, 0)

    def inside(x, carry):
        for i in range(CHUNKS):
            lanes = pl.ds(LANES * i, LANES)
            n = (x + HALO) * CHUNKS + i
            put(n, (0, CY + 8), *halo_rows(y_up[x, :, lanes], y_down[x, :, lanes], row))
            for t in range(CY // 8):
                rows = pl.ds(8 * t, 8)
                put(n, (8 * t + 8,), p[x, rows, lanes], k[x, rows, lanes])
        return carry

    def first(x, carry):
        for r in range(6, 74, 8):
            root, sums = around(s, x, x - 1, x + 1, r, lane)
            centre, total = around(q, x, x - 1, x + 1, r, lane)
            for i in range(CHUNKS):
                scaled = conductance * root[i]
                keep = 1.0 - scaled * sums[i]
                a[x * CHUNKS + i, pl.ds(r, 8), :] = keep
                q1[x * CHUNKS + i, pl.ds(r, 8), :] = keep * centre[i] + (scaled * root[i]) * total[i]
        return carry

    def second(x, carry):
        for r in range(7, 73, 8):
            centre, total = around(q1, x, x - 1, x + 1, r, lane)
            for i in range(CHUNKS):
                root = s[x * CHUNKS + i, pl.ds(r, 8), :]
                keep = a[x * CHUNKS + i, pl.ds(r, 8), :]
                q2[x * CHUNKS + i, pl.ds(r, 8), :] = keep * centre[i] + (conductance * root * root) * total[i]
        return carry

    def third(x, carry):
        for r in range(8, 72, 8):
            centre, total = around(q2, x, x - 1, x + 1, r, lane)
            for i in range(CHUNKS):
                root = s[x * CHUNKS + i, pl.ds(r, 8), :]
                keep = a[x * CHUNKS + i, pl.ds(r, 8), :]
                full[x - HALO, pl.ds(r - 8, 8), pl.ds(LANES * i, LANES)] = (
                    keep * centre[i] / root + (conductance * root) * total[i]
                )
        return carry

    waited(low)
    outside(0, 0)

    def run(begin, end, *stages):
        def step(x, carry):
            for stage, shift in stages:
                stage(x + shift, 0)
            return carry

        lax.fori_loop(begin, end, step, 0)

    t, u, f, c = (third, -3), (second, -1), (first, 1), (inside, 0)
    stores = []
    waited(loads[0])
    run(0, 3, f, c)
    run(3, 4, u, f, c)
    waited(loads[1])
    run(4, 6, u, f, c)
    run(6, 8, t, u, f, c)
    waited(loads[2] + loads[3])
    run(8, 14, t, u, f, c)
    stores += started(pltpu.make_async_copy(full.at[pl.ds(0, 8)], out.at[pl.ds(0, 8)], sems.at[9]))
    run(14, 16, t, u, f, c)
    waited(high)
    outside(1, PLANES - HALO)
    run(16, 20, t, u, f)
    stores += started(pltpu.make_async_copy(full.at[pl.ds(8, 6)], out.at[pl.ds(8, 6)], sems.at[10]))
    run(20, 21, t, u)
    run(21, 22, t)
    stores += started(pltpu.make_async_copy(full.at[pl.ds(14, 2)], out.at[pl.ds(14, 2)], sems.at[11]))
    waited(ask)

    def answer(d, carry):
        value = jnp.zeros((8, LANES), F32)
        for c in range(3):
            cell = asked[d, c]
            x, y, z = cell >> 15, (cell >> 9) & 63, cell & 511
            lanes = pl.ds(pl.multiple_of((z >> 7) * LANES, LANES), LANES)
            tile = full[x, pl.ds(pl.multiple_of((y >> 3) * 8, 8), 8), lanes]
            tile = pltpu.roll(tile, (LANES + c - (z & 127)) & 127, 1)
            value = jnp.where(jnp.logical_and(row == (y & 7), lane == c), tile, value)
        answers[pl.ds(d, 1), :] = jnp.sum(value, axis=0, keepdims=True)
        return carry

    lax.fori_loop(0, NGX, answer, 0, unroll=4)
    waited(stores)


def diffusion(p, k, y_up, y_down, x_up, x_down, cells):
    return pl.pallas_call(
        diffusion_kernel,
        out_shape=(shape(CX, CY, NZ), shape(NGX, LANES)),
        in_specs=[spec(HBM)] * 2 + [spec()] * 2 + [spec(ANY)] * 3,
        out_specs=(spec(HBM), spec()),
        scratch_shapes=[VMEM((PLANES * CHUNKS, ROWS, LANES), F32) for _ in range(5)]
        + [VMEM((CX, CY, NZ), F32) for _ in range(3)]
        + [VMEM((2, 2 * HALO, CY + 8, NZ), F32), pltpu.SMEM((NGX, LANES), jnp.int32), DMA((14,))],
        compiler_params=pltpu.CompilerParams(vmem_limit_bytes=34 << 20),
        cost_estimate=pl.CostEstimate(flops=60_000_000, bytes_accessed=12_000_000, transcendentals=0),
        name="diffusion",
    )(far(p), far(k), y_up, y_down, x_up, x_down, cells)


def friction_kernel(rates, answers, terms, state_out, rate_out):
    known = terms[...]
    state, aged, normal, shear, direct, owners, rank = (known[i : i + 1, 0:TRI] for i in range(7))
    got = answers[...]
    named = lax.broadcasted_iota(jnp.int32, (NGX, TRI), 0).astype(F32) == owners
    held = jnp.zeros((NGX, TRI), F32)
    for c in range(3):
        held = jnp.where(jnp.logical_and(named, rank == float(c)), got[:, c : c + 1], held)
    pressure = jnp.sum(held, axis=0, keepdims=True)
    both = jnp.sum(rates[...], axis=0, keepdims=True)
    first, second = both[:, 0:TRI], both[:, TRI : 2 * TRI]
    effective = normal + step_time * second - pressure
    state_out[...] = state
    rate_out[...] = ((shear + step_time * first) / effective - friction_ref - aged) / direct


def friction(*values):
    return pl.pallas_call(
        friction_kernel,
        out_shape=(shape(1, TRI), shape(1, TRI)),
        in_specs=[spec()] * len(values),
        out_specs=(spec(), spec()),
        compiler_params=pltpu.CompilerParams(vmem_limit_bytes=4 << 20),
        name="friction",
    )(*values)


def exchanged(value, axis):
    return lax.all_to_all(value, axis, split_axis=0, concat_axis=0, tiled=True)


def local(
    pressure,
    permeability,
    kernel,
    slip_rate,
    aging_state,
    normal_stress,
    shear_stress,
    direct_effect,
    evolution_effect,
    slip_distance,
    tri_owner,
    tri_cell,
):
    rows = (
        tri_owner,
        tri_cell,
        slip_rate,
        aging_state,
        normal_stress,
        shear_stress,
        direct_effect,
        evolution_effect,
        slip_distance,
    )
    y_up, y_down, x_up, x_down = pack(pressure, permeability)
    wanted, terms = prepare(*[v.reshape(1, TRI) for v in rows])
    y_up, y_down = lax.ppermute(y_up, "gy", Y_UP), lax.ppermute(y_down, "gy", Y_DOWN)
    lane = lax.broadcasted_iota(jnp.int32, (NGX, LANES), 1)
    row = jnp.pad(lax.ppermute(slip_rate, ("gx", "gy"), SLIP_MOVES), (0, LANES - TRI)).reshape(1, LANES)
    leaving = jnp.where(lane < TRI, row, wanted)
    arrived = exchanged(leaving, "gx")
    x_up, x_down = sides(x_up, x_down, y_up, y_down, leaving)
    x_up, x_down = lax.ppermute(x_up, "gx", X_UP), lax.ppermute(x_down, "gx", X_DOWN)
    partial_sums, cells = partial_rates(arrived, kernel)
    rates = exchanged(partial_sums, "gy")
    field, answers = diffusion(pressure, permeability, y_up, y_down, x_up, x_down, cells)
    answers = exchanged(answers, "gx")
    state_next, log_rate = friction(rates, answers, terms)
    return field, state_next.reshape(TRI), log_rate.reshape(TRI)


def solution(mesh):
    both = P(("gx", "gy"))
    placed = (
        P("gx", "gy", None),
        P("gx", "gy", None),
        P(None, "gx", "gy"),
        *([both] * 7),
        P(("gx", "gy"), None),
        both,
    )
    return jax.shard_map(
        local,
        mesh=mesh,
        in_specs=placed,
        out_specs=(P("gx", "gy", None), both, both),
        check_vma=False,
    )
```

```python
import jax
import jax.numpy as jnp
from jax import lax
from jax.experimental import pallas as pl
from jax.experimental.pallas import tpu as pltpu
from jax.sharding import PartitionSpec as P

NGX, NGY = 32, 8
CX, CY, NZ, TRI = 16, 64, 512, 48
HALO = 3
ROWS = 80
LANES = 128
CHUNKS = NZ // LANES
conductance = 0.15
step_time = 1.0
heal_time = 0.5
friction_ref = 0.6
F32 = jnp.float32
VMEM = pltpu.VMEM
ANY = pl.ANY

X_MOVE = (2, 1, 2, 1, 0, 3, 0, 3)
Y_MOVE = (1, 1, 0, 0, 0, 0, 1, 1)
X_CODE = sum(v << (2 * i) for i, v in enumerate(X_MOVE))
Y_CODE = sum(v << i for i, v in enumerate(Y_MOVE))


def landing(group, other):
    delta = (other - group) & 7
    x = ((group >> 1) + ((X_CODE >> (2 * delta)) & 3)) & 3
    y = (group & 1) ^ ((Y_CODE >> delta) & 1)
    return 2 * x + y


SLIP_MOVES = [
    ((4 * g + r) * NGY + j, (4 * landing(g, j) + r) * NGY + g) for g in range(8) for r in range(4) for j in range(NGY)
]
X_UP = [(i, i + 1) for i in range(NGX - 1)]
X_DOWN = [(j, i) for i, j in X_UP]
Y_UP = [(i, i + 1) for i in range(NGY - 1)]
Y_DOWN = [(j, i) for i, j in Y_UP]


def spec(space=VMEM):
    return pl.BlockSpec(memory_space=space)


def shape(*dims, dtype=F32):
    return jax.ShapeDtypeStruct(dims, dtype)


def far(value):
    return pltpu.with_memory_space_constraint(value, pltpu.HBM)


def all_far(*values):
    return tuple(far(v) for v in values)


def started(*copies):
    for copy in copies:
        copy.start()
    return copies


def waited(copies):
    for copy in copies:
        copy.wait()


HBM = pltpu.HBM
DMA = pltpu.SemaphoreType.DMA


def turned(row_value):
    row = lax.broadcasted_iota(jnp.int32, (TRI, TRI), 0)
    column = lax.broadcasted_iota(jnp.int32, (TRI, TRI), 1)
    return jnp.sum(jnp.where(row == column, row_value, 0.0), axis=1, keepdims=True)


def pack_kernel(p, k, y_up, y_down, x_up, x_down, tiles, rows, sems):
    tops = started(
        pltpu.make_async_copy(p.at[:, pl.ds(CY - 8, 8), :], tiles.at[0], sems.at[0]),
        pltpu.make_async_copy(k.at[:, pl.ds(CY - 8, 8), :], tiles.at[1], sems.at[1]),
        pltpu.make_async_copy(p.at[:, pl.ds(0, 8), :], tiles.at[2], sems.at[2]),
        pltpu.make_async_copy(k.at[:, pl.ds(0, 8), :], tiles.at[3], sems.at[3]),
    )
    loads = [
        started(
            *[
                pltpu.make_async_copy(
                    source.at[pl.ds(start, HALO)], rows.at[side, pl.ds(HALO * n, HALO)], sems.at[4 + 2 * side + n]
                )
                for n, source in enumerate((p, k))
            ]
        )
        for side, start in enumerate((CX - HALO, 0))
    ]
    row = lax.broadcasted_iota(jnp.int32, (8, NZ), 0)
    waited(tops)

    def plane(x, carry):
        y_up[x] = jnp.where(row >= 5, tiles[0, x], pltpu.roll(tiles[1, x], 3, 0))
        y_down[x] = jnp.where(row < 3, tiles[2, x], pltpu.roll(tiles[3, x], 5, 0))
        return carry

    lax.fori_loop(0, CX, plane, 0)
    stores = []
    for side, target in enumerate((x_up, x_down)):
        waited(loads[side])
        stores += started(pltpu.make_async_copy(rows.at[side], target.at[:, pl.ds(0, CY)], sems.at[8 + side]))
    waited(stores)


def pack(p, k):
    return pl.pallas_call(
        pack_kernel,
        out_shape=(shape(CX, 8, NZ),) * 2 + (HBM((2 * HALO, CY + 8, NZ), F32),) * 2,
        in_specs=[spec(HBM)] * 2,
        out_specs=(spec(),) * 2 + (spec(HBM),) * 2,
        scratch_shapes=[VMEM((4, CX, 8, NZ), F32), VMEM((2, 2 * HALO, CY, NZ), F32), DMA((10,))],
        compiler_params=pltpu.CompilerParams(vmem_limit_bytes=6 << 20),
        name="pack",
    )(far(p), far(k))


def prepare_kernel(moved, owner, cell, *refs):
    floats, (leaving, terms, whole, held, sems) = refs[:7], refs[7:]
    waited(
        started(
            pltpu.make_async_copy(owner, whole.at[0], sems.at[0]),
            pltpu.make_async_copy(cell, whole.at[1], sems.at[1]),
            *[pltpu.make_async_copy(ref, held.at[n], sems.at[2 + n]) for n, ref in enumerate(floats)],
        )
    )
    slip, aging, normal, shear, direct, evolution, distance = (held[n] for n in range(7))
    owners = whole[0].astype(F32)
    first = lax.broadcasted_iota(jnp.int32, (TRI, TRI), 0)
    second = lax.broadcasted_iota(jnp.int32, (TRI, TRI), 1)
    same = jnp.logical_and(turned(owners) == owners, first < second)
    rank = jnp.sum(jnp.where(same, 1.0, 0.0), axis=0, keepdims=True)
    cells = whole[1].astype(F32)
    lane = lax.broadcasted_iota(jnp.int32, (NGX, LANES), 1)
    named = lax.broadcasted_iota(jnp.int32, (NGX, TRI), 0) == whole[0]
    value = jnp.zeros((NGX, LANES), F32)
    for c in range(3):
        asked = jnp.where(jnp.logical_and(named, rank == float(c)), cells, 0.0)
        value = jnp.where(lane == TRI + c, jnp.sum(asked, axis=1, keepdims=True), value)
    leaving[...] = value
    leaving[:, 0:TRI] = jnp.broadcast_to(moved[...], (NGX, TRI))
    ratio = distance / slip
    state = ratio + (aging - ratio) * jnp.exp(-heal_time / ratio)
    terms[...] = jnp.zeros((8, LANES), F32)
    aged = evolution * jnp.log(state / distance)
    for n, term in enumerate((state, aged, normal, shear, direct, owners, rank)):
        terms[n : n + 1, 0:TRI] = term


def prepare(moved, *values):
    return pl.pallas_call(
        prepare_kernel,
        out_shape=(shape(NGX, LANES), shape(8, LANES)),
        in_specs=[spec()] + [spec(HBM)] * len(values),
        out_specs=(spec(),) * 2,
        scratch_shapes=[VMEM((2, 1, TRI), jnp.int32), VMEM((7, 1, TRI), F32), DMA((9,))],
        compiler_params=pltpu.CompilerParams(vmem_limit_bytes=2 << 20),
        cost_estimate=pl.CostEstimate(flops=10**12, bytes_accessed=0, transcendentals=0),
        name="prepare",
    )(moved, *all_far(*values))


def halo_rows(low, high, row):
    p = jnp.where(row >= 5, low, jnp.where(row < 3, high, 0.0))
    k = jnp.where(row >= 5, pltpu.roll(low, 5, 0), jnp.where(row < 3, pltpu.roll(high, 3, 0), 0.0))
    return p, k


def sides_kernel(x_up, x_down, y_up, y_down, token, x_up_out, x_down_out, tiles, sems):
    del x_up, x_down, token
    row = lax.broadcasted_iota(jnp.int32, (8, NZ), 0)
    copies = []
    for side, (target, start) in enumerate(((x_up_out, CX - HALO), (x_down_out, 0))):
        for n in range(HALO):
            tiles[side, n], tiles[side, HALO + n] = halo_rows(y_up[start + n], y_down[start + n], row)
        copies += started(pltpu.make_async_copy(tiles.at[side], target.at[:, pl.ds(CY, 8)], sems.at[side]))
    waited(copies)


def sides(x_up, x_down, y_up, y_down, token):
    return pl.pallas_call(
        sides_kernel,
        out_shape=(HBM((2 * HALO, CY + 8, NZ), F32),) * 2,
        in_specs=[spec(HBM)] * 2 + [spec()] * 2 + [spec(ANY)],
        out_specs=(spec(HBM),) * 2,
        scratch_shapes=[VMEM((2, 2 * HALO, 8, NZ), F32), DMA((2,))],
        input_output_aliases={0: 0, 1: 1},
        compiler_params=pltpu.CompilerParams(vmem_limit_bytes=4 << 20),
        name="sides",
    )(far(x_up), far(x_down), y_up, y_down, token)


def rates_kernel(arrived, kernel_far, out, cells, acc, kernel, sems):
    copies = started(
        *[
            pltpu.make_async_copy(
                kernel_far.at[n // 4, pl.ds(96 * (n % 4), 96)], kernel.at[n // 4, pl.ds(96 * (n % 4), 96)], sems.at[n]
            )
            for n in range(8)
        ]
    )
    gy = lax.axis_index("gy")
    lane = lax.broadcasted_iota(jnp.int32, (1, LANES), 1)
    chunks = [jnp.zeros((1, LANES), F32) for _ in range(12)]
    for j in range(NGY):
        spot = landing(gy, j)
        for r in range(4):
            start = (r * NGY + j) * TRI
            chunk, offset = divmod(start, LANES)
            row = pltpu.roll(arrived[pl.ds(4 * spot + r, 1), :], offset, 1)
            inside = jnp.logical_and(lane >= offset, lane < offset + TRI)
            chunks[chunk] = jnp.where(inside, row, chunks[chunk])
            if offset + TRI > LANES:
                chunks[chunk + 1] = jnp.where(lane < offset + TRI - LANES, row, chunks[chunk + 1])
    cells[...] = pltpu.roll(arrived[...], LANES - TRI, 1).astype(jnp.int32)
    wide = [jnp.broadcast_to(c, (8, LANES)) for c in chunks]

    for n in range(8):
        part = n // 4
        copies[n].wait()

        def tile(t, carry):
            rows = pl.ds(pl.multiple_of(t * 8, 8), 8)
            terms = [kernel[part, rows, pl.ds(LANES * c, LANES)] * wide[c] for c in range(12)]
            while len(terms) > 1:
                terms = [a + b for a, b in zip(terms[::2], terms[1::2])] + terms[len(terms) // 2 * 2 :]
            dest = (t // 6) * 96 + part * TRI + (t % 6) * 8
            acc[pl.ds(pl.multiple_of(dest, 8), 8), :] = terms[0]
            return carry

        lax.fori_loop(12 * (n % 4), 12 * (n % 4) + 12, tile, 0, unroll=4)
    row8 = lax.broadcasted_iota(jnp.int32, (8, LANES), 0)
    total = jnp.zeros((8, 2 * TRI), F32)
    for j in range(NGY):
        total = total + lax.dot_general(
            jnp.where(row8 == j, 1.0, 0.0),
            acc[pl.ds(2 * TRI * j, 2 * TRI), :],
            (((1,), (1,)), ((), ())),
            precision=lax.Precision.HIGHEST,
            preferred_element_type=F32,
        )
    out[...] = jnp.zeros((8, LANES), F32)
    out[:, 0 : 2 * TRI] = total


def partial_rates(arrived, kernel):
    return pl.pallas_call(
        rates_kernel,
        out_shape=(shape(NGY, LANES), shape(NGX, LANES, dtype=jnp.int32)),
        in_specs=[spec(), spec(HBM)],
        out_specs=(spec(), spec()),
        scratch_shapes=[VMEM((768, LANES), F32), VMEM(kernel.shape, F32), DMA((8,))],
        compiler_params=pltpu.CompilerParams(vmem_limit_bytes=8 << 20),
        cost_estimate=pl.CostEstimate(flops=1000000000000, bytes_accessed=6000000000, transcendentals=0),
        name="rates",
    )(arrived, far(kernel))


def around(ref, x, before, after, row, lane):
    rows = pl.ds(row, 8)
    centre = [ref[x * CHUNKS + i, rows, :] for i in range(CHUNKS)]
    left = [pltpu.roll(v, 1, 1) for v in centre]
    right = [pltpu.roll(v, LANES - 1, 1) for v in centre]
    sums = []
    for i in range(CHUNKS):
        below = left[i - 1] if i else 0.0
        above = right[i + 1] if i + 1 < CHUNKS else 0.0
        z = jnp.where(lane == 0, below, left[i]) + jnp.where(lane == LANES - 1, above, right[i])
        y = ref[x * CHUNKS + i, pl.ds(row - 1, 8), :] + ref[x * CHUNKS + i, pl.ds(row + 1, 8), :]
        xs = ref[before * CHUNKS + i, rows, :] + ref[after * CHUNKS + i, rows, :]
        sums.append((xs + y) + z)
    return centre, sums


PLANES = CX + 2 * HALO


def diffusion_kernel(
    p_far, k_far, y_up, y_down, x_up, x_down, cells, out, answers, s, q, a, q1, q2, p, k, full, wide, asked, sems
):
    loads = []
    low = started(pltpu.make_async_copy(x_up, wide.at[0], sems.at[12]))
    for n in range(4):
        planes = pl.ds(4 * n, 4)
        loads.append(
            started(
                pltpu.make_async_copy(p_far.at[planes], p.at[planes], sems.at[2 * n]),
                pltpu.make_async_copy(k_far.at[planes], k.at[planes], sems.at[2 * n + 1]),
            )
        )
    high = started(pltpu.make_async_copy(x_down, wide.at[1], sems.at[13]))
    ask = started(pltpu.make_async_copy(cells, asked, sems.at[8]))
    lane = lax.broadcasted_iota(jnp.int32, (8, LANES), 1)
    row = lax.broadcasted_iota(jnp.int32, (8, LANES), 0)

    def put(n, places, p_tile, k_tile):
        root = jnp.sqrt(k_tile)
        scaled = root * p_tile
        for place in places:
            s[n, place : place + 8, :] = root
            q[n, place : place + 8, :] = scaled

    def outside(side, base):
        def plane(n, carry):
            for i in range(CHUNKS):
                lanes = pl.ds(LANES * i, LANES)
                for t in range(CY // 8 + 1):
                    places = (8 * t + 8,) if t < CY // 8 else (0, CY + 8)
                    rows = pl.ds(8 * t, 8)
                    put((base + n) * CHUNKS + i, places, wide[side, n, rows, lanes], wide[side, HALO + n, rows, lanes])
            return carry

        lax.fori_loop(0, HALO, plane, 0)

    def inside(x, carry):
        for i in range(CHUNKS):
            lanes = pl.ds(LANES * i, LANES)
            n = (x + HALO) * CHUNKS + i
            put(n, (0, CY + 8), *halo_rows(y_up[x, :, lanes], y_down[x, :, lanes], row))
            for t in range(CY // 8):
                rows = pl.ds(8 * t, 8)
                put(n, (8 * t + 8,), p[x, rows, lanes], k[x, rows, lanes])
        return carry

    def first(x, carry):
        for r in range(6, 74, 8):
            root, sums = around(s, x, x - 1, x + 1, r, lane)
            centre, total = around(q, x, x - 1, x + 1, r, lane)
            for i in range(CHUNKS):
                scaled = conductance * root[i]
                keep = 1.0 - scaled * sums[i]
                a[x * CHUNKS + i, pl.ds(r, 8), :] = keep
                q1[x * CHUNKS + i, pl.ds(r, 8), :] = keep * centre[i] + (scaled * root[i]) * total[i]
        return carry

    def second(x, carry):
        for r in range(7, 73, 8):
            centre, total = around(q1, x, x - 1, x + 1, r, lane)
            for i in range(CHUNKS):
                root = s[x * CHUNKS + i, pl.ds(r, 8), :]
                keep = a[x * CHUNKS + i, pl.ds(r, 8), :]
                q2[x * CHUNKS + i, pl.ds(r, 8), :] = keep * centre[i] + (conductance * root * root) * total[i]
        return carry

    def third(x, carry):
        for r in range(8, 72, 8):
            centre, total = around(q2, x, x - 1, x + 1, r, lane)
            for i in range(CHUNKS):
                root = s[x * CHUNKS + i, pl.ds(r, 8), :]
                keep = a[x * CHUNKS + i, pl.ds(r, 8), :]
                full[x - HALO, pl.ds(r - 8, 8), pl.ds(LANES * i, LANES)] = (
                    keep * centre[i] / root + (conductance * root) * total[i]
                )
        return carry

    waited(low)
    outside(0, 0)

    def run(begin, end, *stages):
        def step(x, carry):
            for stage, shift in stages:
                stage(x + shift, 0)
            return carry

        lax.fori_loop(begin, end, step, 0)

    t, u, f, c = (third, -3), (second, -1), (first, 1), (inside, 0)
    stores = []
    waited(loads[0])
    run(0, 3, f, c)
    run(3, 4, u, f, c)
    waited(loads[1])
    run(4, 6, u, f, c)
    run(6, 8, t, u, f, c)
    waited(loads[2] + loads[3])
    run(8, 14, t, u, f, c)
    stores += started(pltpu.make_async_copy(full.at[pl.ds(0, 8)], out.at[pl.ds(0, 8)], sems.at[9]))
    run(14, 16, t, u, f, c)
    waited(high)
    outside(1, PLANES - HALO)
    run(16, 20, t, u, f)
    stores += started(pltpu.make_async_copy(full.at[pl.ds(8, 6)], out.at[pl.ds(8, 6)], sems.at[10]))
    run(20, 21, t, u)
    run(21, 22, t)
    stores += started(pltpu.make_async_copy(full.at[pl.ds(14, 2)], out.at[pl.ds(14, 2)], sems.at[11]))
    waited(ask)

    def answer(d, carry):
        value = jnp.zeros((8, LANES), F32)
        for c in range(3):
            cell = asked[d, c]
            x, y, z = cell >> 15, (cell >> 9) & 63, cell & 511
            lanes = pl.ds(pl.multiple_of((z >> 7) * LANES, LANES), LANES)
            tile = full[x, pl.ds(pl.multiple_of((y >> 3) * 8, 8), 8), lanes]
            tile = pltpu.roll(tile, (LANES + c - (z & 127)) & 127, 1)
            value = jnp.where(jnp.logical_and(row == (y & 7), lane == c), tile, value)
        answers[pl.ds(d, 1), :] = jnp.sum(value, axis=0, keepdims=True)
        return carry

    lax.fori_loop(0, NGX, answer, 0, unroll=4)
    waited(stores)


def diffusion(p, k, y_up, y_down, x_up, x_down, cells):
    return pl.pallas_call(
        diffusion_kernel,
        out_shape=(shape(CX, CY, NZ), shape(NGX, LANES)),
        in_specs=[spec(HBM)] * 2 + [spec()] * 2 + [spec(ANY)] * 3,
        out_specs=(spec(HBM), spec()),
        scratch_shapes=[VMEM((PLANES * CHUNKS, ROWS, LANES), F32) for _ in range(5)]
        + [VMEM((CX, CY, NZ), F32) for _ in range(3)]
        + [VMEM((2, 2 * HALO, CY + 8, NZ), F32), pltpu.SMEM((NGX, LANES), jnp.int32), DMA((14,))],
        compiler_params=pltpu.CompilerParams(vmem_limit_bytes=34 << 20),
        cost_estimate=pl.CostEstimate(flops=60_000_000, bytes_accessed=12_000_000, transcendentals=0),
        name="diffusion",
    )(far(p), far(k), y_up, y_down, x_up, x_down, cells)


def friction_kernel(rates, answers, terms, state_out, rate_out):
    known = terms[...]
    state, aged, normal, shear, direct, owners, rank = (known[i : i + 1, 0:TRI] for i in range(7))
    got = answers[...]
    named = lax.broadcasted_iota(jnp.int32, (NGX, TRI), 0).astype(F32) == owners
    held = jnp.zeros((NGX, TRI), F32)
    for c in range(3):
        held = jnp.where(jnp.logical_and(named, rank == float(c)), got[:, c : c + 1], held)
    pressure = jnp.sum(held, axis=0, keepdims=True)
    both = jnp.sum(rates[...], axis=0, keepdims=True)
    first, second = both[:, 0:TRI], both[:, TRI : 2 * TRI]
    effective = normal + step_time * second - pressure
    state_out[...] = state
    rate_out[...] = ((shear + step_time * first) / effective - friction_ref - aged) / direct


def friction(*values):
    return pl.pallas_call(
        friction_kernel,
        out_shape=(shape(1, TRI), shape(1, TRI)),
        in_specs=[spec()] * len(values),
        out_specs=(spec(), spec()),
        compiler_params=pltpu.CompilerParams(vmem_limit_bytes=4 << 20),
        name="friction",
    )(*values)


def exchanged(value, axis):
    return lax.all_to_all(value, axis, split_axis=0, concat_axis=0, tiled=True)


def local(
    pressure,
    permeability,
    kernel,
    slip_rate,
    aging_state,
    normal_stress,
    shear_stress,
    direct_effect,
    evolution_effect,
    slip_distance,
    tri_owner,
    tri_cell,
):
    rows = (
        tri_owner,
        tri_cell,
        slip_rate,
        aging_state,
        normal_stress,
        shear_stress,
        direct_effect,
        evolution_effect,
        slip_distance,
    )
    y_up, y_down, x_up, x_down = pack(pressure, permeability)
    moved = lax.ppermute(slip_rate, ("gx", "gy"), SLIP_MOVES).reshape(1, TRI)
    leaving, terms = prepare(moved, *[v.reshape(1, TRI) for v in rows])
    y_up, y_down = lax.ppermute(y_up, "gy", Y_UP), lax.ppermute(y_down, "gy", Y_DOWN)
    arrived = exchanged(leaving, "gx")
    x_up, x_down = sides(x_up, x_down, y_up, y_down, leaving)
    x_up, x_down = lax.ppermute(x_up, "gx", X_UP), lax.ppermute(x_down, "gx", X_DOWN)
    partial_sums, cells = partial_rates(arrived, kernel)
    rates = exchanged(partial_sums, "gy")
    field, answers = diffusion(pressure, permeability, y_up, y_down, x_up, x_down, cells)
    answers = exchanged(answers, "gx")
    state_next, log_rate = friction(rates, answers, terms)
    return field, state_next.reshape(TRI), log_rate.reshape(TRI)


def solution(mesh):
    both = P(("gx", "gy"))
    placed = (
        P("gx", "gy", None),
        P("gx", "gy", None),
        P(None, "gx", "gy"),
        *([both] * 7),
        P(("gx", "gy"), None),
        both,
    )
    return jax.shard_map(
        local,
        mesh=mesh,
        in_specs=placed,
        out_specs=(P("gx", "gy", None), both, both),
        check_vma=False,
    )
```

```python
import jax
import jax.numpy as jnp
from jax import lax
from jax.experimental import pallas as pl
from jax.experimental.pallas import tpu as pltpu
from jax.sharding import PartitionSpec as P

NGX, NGY = 32, 8
CX, CY, NZ, TRI = 16, 64, 512, 48
HALO = 3
ROWS = 80
LANES = 128
CHUNKS = NZ // LANES
conductance = 0.15
step_time = 1.0
heal_time = 0.5
friction_ref = 0.6
F32 = jnp.float32
VMEM = pltpu.VMEM
ANY = pl.ANY

X_MOVE = (2, 1, 2, 1, 0, 3, 0, 3)
Y_MOVE = (1, 1, 0, 0, 0, 0, 1, 1)
X_CODE = sum(v << (2 * i) for i, v in enumerate(X_MOVE))
Y_CODE = sum(v << i for i, v in enumerate(Y_MOVE))


def landing(group, other):
    delta = (other - group) & 7
    x = ((group >> 1) + ((X_CODE >> (2 * delta)) & 3)) & 3
    y = (group & 1) ^ ((Y_CODE >> delta) & 1)
    return 2 * x + y


SLIP_MOVES = [
    ((4 * g + r) * NGY + j, (4 * landing(g, j) + r) * NGY + g) for g in range(8) for r in range(4) for j in range(NGY)
]
X_FAR = [pair for i in range(1, NGX - 1, 2) for pair in ((i, i + 1), (i + 1, i))]
X_NEAR = [pair for i in range(0, NGX, 2) for pair in ((i, i + 1), (i + 1, i))]
Y_UP = [(i, i + 1) for i in range(NGY - 1)]
Y_DOWN = [(j, i) for i, j in Y_UP]


def spec(space=VMEM):
    return pl.BlockSpec(memory_space=space)


def shape(*dims, dtype=F32):
    return jax.ShapeDtypeStruct(dims, dtype)


def far(value):
    return pltpu.with_memory_space_constraint(value, pltpu.HBM)


def all_far(*values):
    return tuple(far(v) for v in values)


def core():
    return lax.rem(lax.axis_index("gx"), 2)


def sent_planes(core_index):
    return (CX - HALO) * core_index, (CX - HALO) * (1 - core_index)


def started(*copies):
    for copy in copies:
        copy.start()
    return copies


def waited(copies):
    for copy in copies:
        copy.wait()


HBM = pltpu.HBM
DMA = pltpu.SemaphoreType.DMA


def turned(row_value):
    row = lax.broadcasted_iota(jnp.int32, (TRI, TRI), 0)
    column = lax.broadcasted_iota(jnp.int32, (TRI, TRI), 1)
    return jnp.sum(jnp.where(row == column, row_value, 0.0), axis=1, keepdims=True)


def pack_kernel(p, k, y_up, y_down, x_far, x_near, tiles, rows, sems):
    tops = started(
        pltpu.make_async_copy(p.at[:, pl.ds(CY - 8, 8), :], tiles.at[0], sems.at[0]),
        pltpu.make_async_copy(k.at[:, pl.ds(CY - 8, 8), :], tiles.at[1], sems.at[1]),
        pltpu.make_async_copy(p.at[:, pl.ds(0, 8), :], tiles.at[2], sems.at[2]),
        pltpu.make_async_copy(k.at[:, pl.ds(0, 8), :], tiles.at[3], sems.at[3]),
    )
    loads = [
        started(
            *[
                pltpu.make_async_copy(
                    source.at[pl.ds(start, HALO)], rows.at[side, pl.ds(HALO * n, HALO)], sems.at[4 + 2 * side + n]
                )
                for n, source in enumerate((p, k))
            ]
        )
        for side, start in enumerate(sent_planes(core()))
    ]
    row = lax.broadcasted_iota(jnp.int32, (8, NZ), 0)
    waited(tops)

    def plane(x, carry):
        y_up[x] = jnp.where(row >= 5, tiles[0, x], pltpu.roll(tiles[1, x], 3, 0))
        y_down[x] = jnp.where(row < 3, tiles[2, x], pltpu.roll(tiles[3, x], 5, 0))
        return carry

    lax.fori_loop(0, CX, plane, 0)
    stores = []
    for side, target in enumerate((x_far, x_near)):
        waited(loads[side])
        stores += started(pltpu.make_async_copy(rows.at[side], target.at[:, pl.ds(0, CY)], sems.at[8 + side]))
    waited(stores)


def pack(p, k):
    return pl.pallas_call(
        pack_kernel,
        out_shape=(shape(CX, 8, NZ),) * 2 + (HBM((2 * HALO, CY + 8, NZ), F32),) * 2,
        in_specs=[spec(HBM)] * 2,
        out_specs=(spec(),) * 2 + (spec(HBM),) * 2,
        scratch_shapes=[VMEM((4, CX, 8, NZ), F32), VMEM((2, 2 * HALO, CY, NZ), F32), DMA((10,))],
        compiler_params=pltpu.CompilerParams(vmem_limit_bytes=6 << 20),
        name="pack",
    )(far(p), far(k))


def prepare_kernel(owner, cell, *refs):
    floats, (wanted, terms, whole, held, sems) = refs[:7], refs[7:]
    waited(
        started(
            pltpu.make_async_copy(owner, whole.at[0], sems.at[0]),
            pltpu.make_async_copy(cell, whole.at[1], sems.at[1]),
            *[pltpu.make_async_copy(ref, held.at[n], sems.at[2 + n]) for n, ref in enumerate(floats)],
        )
    )
    slip, aging, normal, shear, direct, evolution, distance = (held[n] for n in range(7))
    owners = whole[0].astype(F32)
    first = lax.broadcasted_iota(jnp.int32, (TRI, TRI), 0)
    second = lax.broadcasted_iota(jnp.int32, (TRI, TRI), 1)
    same = jnp.logical_and(turned(owners) == owners, first < second)
    rank = jnp.sum(jnp.where(same, 1.0, 0.0), axis=0, keepdims=True)
    cells = whole[1].astype(F32)
    lane = lax.broadcasted_iota(jnp.int32, (NGX, LANES), 1)
    named = lax.broadcasted_iota(jnp.int32, (NGX, TRI), 0) == whole[0]
    value = jnp.zeros((NGX, LANES), F32)
    for c in range(3):
        asked = jnp.where(jnp.logical_and(named, rank == float(c)), cells, 0.0)
        value = jnp.where(lane == TRI + c, jnp.sum(asked, axis=1, keepdims=True), value)
    wanted[...] = value
    ratio = distance / slip
    state = ratio + (aging - ratio) * jnp.exp(-heal_time / ratio)
    terms[...] = jnp.zeros((8, LANES), F32)
    aged = evolution * jnp.log(state / distance)
    for n, term in enumerate((state, aged, normal, shear, direct, owners, rank)):
        terms[n : n + 1, 0:TRI] = term


def prepare(*values):
    return pl.pallas_call(
        prepare_kernel,
        out_shape=(shape(NGX, LANES), shape(8, LANES)),
        in_specs=[spec(HBM)] * len(values),
        out_specs=(spec(),) * 2,
        scratch_shapes=[VMEM((2, 1, TRI), jnp.int32), VMEM((7, 1, TRI), F32), DMA((9,))],
        compiler_params=pltpu.CompilerParams(vmem_limit_bytes=2 << 20),
        name="prepare",
    )(*all_far(*values))


def halo_rows(low, high, row):
    p = jnp.where(row >= 5, low, jnp.where(row < 3, high, 0.0))
    k = jnp.where(row >= 5, pltpu.roll(low, 5, 0), jnp.where(row < 3, pltpu.roll(high, 3, 0), 0.0))
    return p, k


def sides_kernel(x_far, x_near, y_up, y_down, token, x_far_out, x_near_out, tiles, sems):
    del x_far, x_near, token
    row = lax.broadcasted_iota(jnp.int32, (8, NZ), 0)
    copies = []
    for side, (target, start) in enumerate(zip((x_far_out, x_near_out), sent_planes(core()))):
        for n in range(HALO):
            tiles[side, n], tiles[side, HALO + n] = halo_rows(y_up[start + n], y_down[start + n], row)
        copies += started(pltpu.make_async_copy(tiles.at[side], target.at[:, pl.ds(CY, 8)], sems.at[side]))
    waited(copies)


def sides(x_far, x_near, y_up, y_down, token):
    return pl.pallas_call(
        sides_kernel,
        out_shape=(HBM((2 * HALO, CY + 8, NZ), F32),) * 2,
        in_specs=[spec(HBM)] * 2 + [spec()] * 2 + [spec(ANY)],
        out_specs=(spec(HBM),) * 2,
        scratch_shapes=[VMEM((2, 2 * HALO, 8, NZ), F32), DMA((2,))],
        input_output_aliases={0: 0, 1: 1},
        compiler_params=pltpu.CompilerParams(vmem_limit_bytes=4 << 20),
        name="sides",
    )(far(x_far), far(x_near), y_up, y_down, token)


def rates_kernel(arrived, kernel_far, out, cells, acc, kernel, sems):
    copies = started(
        *[
            pltpu.make_async_copy(
                kernel_far.at[n // 4, pl.ds(96 * (n % 4), 96)], kernel.at[n // 4, pl.ds(96 * (n % 4), 96)], sems.at[n]
            )
            for n in range(8)
        ]
    )
    gy = lax.axis_index("gy")
    lane = lax.broadcasted_iota(jnp.int32, (1, LANES), 1)
    chunks = [jnp.zeros((1, LANES), F32) for _ in range(12)]
    for j in range(NGY):
        spot = landing(gy, j)
        for r in range(4):
            start = (r * NGY + j) * TRI
            chunk, offset = divmod(start, LANES)
            row = pltpu.roll(arrived[pl.ds(4 * spot + r, 1), :], offset, 1)
            inside = jnp.logical_and(lane >= offset, lane < offset + TRI)
            chunks[chunk] = jnp.where(inside, row, chunks[chunk])
            if offset + TRI > LANES:
                chunks[chunk + 1] = jnp.where(lane < offset + TRI - LANES, row, chunks[chunk + 1])
    cells[...] = pltpu.roll(arrived[...], LANES - TRI, 1).astype(jnp.int32)
    wide = [jnp.broadcast_to(c, (8, LANES)) for c in chunks]

    for n in range(8):
        part = n // 4
        copies[n].wait()

        def tile(t, carry):
            rows = pl.ds(pl.multiple_of(t * 8, 8), 8)
            terms = [kernel[part, rows, pl.ds(LANES * c, LANES)] * wide[c] for c in range(12)]
            while len(terms) > 1:
                terms = [a + b for a, b in zip(terms[::2], terms[1::2])] + terms[len(terms) // 2 * 2 :]
            dest = (t // 6) * 96 + part * TRI + (t % 6) * 8
            acc[pl.ds(pl.multiple_of(dest, 8), 8), :] = terms[0]
            return carry

        lax.fori_loop(12 * (n % 4), 12 * (n % 4) + 12, tile, 0, unroll=4)
    row8 = lax.broadcasted_iota(jnp.int32, (8, LANES), 0)
    total = jnp.zeros((8, 2 * TRI), F32)
    for j in range(NGY):
        total = total + lax.dot_general(
            jnp.where(row8 == j, 1.0, 0.0),
            acc[pl.ds(2 * TRI * j, 2 * TRI), :],
            (((1,), (1,)), ((), ())),
            precision=lax.Precision.HIGHEST,
            preferred_element_type=F32,
        )
    out[...] = jnp.zeros((8, LANES), F32)
    out[:, 0 : 2 * TRI] = total


def partial_rates(arrived, kernel):
    return pl.pallas_call(
        rates_kernel,
        out_shape=(shape(NGY, LANES), shape(NGX, LANES, dtype=jnp.int32)),
        in_specs=[spec(), spec(HBM)],
        out_specs=(spec(), spec()),
        scratch_shapes=[VMEM((768, LANES), F32), VMEM(kernel.shape, F32), DMA((8,))],
        compiler_params=pltpu.CompilerParams(vmem_limit_bytes=8 << 20),
        cost_estimate=pl.CostEstimate(flops=1000000000000, bytes_accessed=6000000000, transcendentals=0),
        name="rates",
    )(arrived, far(kernel))


def around(ref, x, before, after, row, lane):
    rows = pl.ds(row, 8)
    centre = [ref[x * CHUNKS + i, rows, :] for i in range(CHUNKS)]
    left = [pltpu.roll(v, 1, 1) for v in centre]
    right = [pltpu.roll(v, LANES - 1, 1) for v in centre]
    sums = []
    for i in range(CHUNKS):
        below = left[i - 1] if i else 0.0
        above = right[i + 1] if i + 1 < CHUNKS else 0.0
        z = jnp.where(lane == 0, below, left[i]) + jnp.where(lane == LANES - 1, above, right[i])
        y = ref[x * CHUNKS + i, pl.ds(row - 1, 8), :] + ref[x * CHUNKS + i, pl.ds(row + 1, 8), :]
        xs = ref[before * CHUNKS + i, rows, :] + ref[after * CHUNKS + i, rows, :]
        sums.append((xs + y) + z)
    return centre, sums


PLANES = CX + 2 * HALO


def diffusion_kernel(
    p_far, k_far, y_up, y_down, x_far, x_near, cells, out, answers, s, q, a, q1, q2, p, k, full, wide, asked, sems
):
    loads = []
    odd = core()
    started(pltpu.make_async_copy(x_far, wide.at[odd], sems.at[12 + odd]))
    started(pltpu.make_async_copy(x_near, wide.at[1 - odd], sems.at[13 - odd]))
    for n in range(4):
        planes = pl.ds(4 * n, 4)
        loads.append(
            started(
                pltpu.make_async_copy(p_far.at[planes], p.at[planes], sems.at[2 * n]),
                pltpu.make_async_copy(k_far.at[planes], k.at[planes], sems.at[2 * n + 1]),
            )
        )
    low = [pltpu.make_async_copy(x_far, wide.at[0], sems.at[12])]
    high = [pltpu.make_async_copy(x_near, wide.at[1], sems.at[13])]
    ask = started(pltpu.make_async_copy(cells, asked, sems.at[8]))
    lane = lax.broadcasted_iota(jnp.int32, (8, LANES), 1)
    row = lax.broadcasted_iota(jnp.int32, (8, LANES), 0)

    def put(n, places, p_tile, k_tile):
        root = jnp.sqrt(k_tile)
        scaled = root * p_tile
        for place in places:
            s[n, place : place + 8, :] = root
            q[n, place : place + 8, :] = scaled

    def outside(side, base):
        def plane(n, carry):
            for i in range(CHUNKS):
                lanes = pl.ds(LANES * i, LANES)
                for t in range(CY // 8 + 1):
                    places = (8 * t + 8,) if t < CY // 8 else (0, CY + 8)
                    rows = pl.ds(8 * t, 8)
                    put((base + n) * CHUNKS + i, places, wide[side, n, rows, lanes], wide[side, HALO + n, rows, lanes])
            return carry

        lax.fori_loop(0, HALO, plane, 0)

    def inside(x, carry):
        for i in range(CHUNKS):
            lanes = pl.ds(LANES * i, LANES)
            n = (x + HALO) * CHUNKS + i
            put(n, (0, CY + 8), *halo_rows(y_up[x, :, lanes], y_down[x, :, lanes], row))
            for t in range(CY // 8):
                rows = pl.ds(8 * t, 8)
                put(n, (8 * t + 8,), p[x, rows, lanes], k[x, rows, lanes])
        return carry

    def first(x, carry):
        for r in range(6, 74, 8):
            root, sums = around(s, x, x - 1, x + 1, r, lane)
            centre, total = around(q, x, x - 1, x + 1, r, lane)
            for i in range(CHUNKS):
                scaled = conductance * root[i]
                keep = 1.0 - scaled * sums[i]
                a[x * CHUNKS + i, pl.ds(r, 8), :] = keep
                q1[x * CHUNKS + i, pl.ds(r, 8), :] = keep * centre[i] + (scaled * root[i]) * total[i]
        return carry

    def second(x, carry):
        for r in range(7, 73, 8):
            centre, total = around(q1, x, x - 1, x + 1, r, lane)
            for i in range(CHUNKS):
                root = s[x * CHUNKS + i, pl.ds(r, 8), :]
                keep = a[x * CHUNKS + i, pl.ds(r, 8), :]
                q2[x * CHUNKS + i, pl.ds(r, 8), :] = keep * centre[i] + (conductance * root * root) * total[i]
        return carry

    def third(x, carry):
        for r in range(8, 72, 8):
            centre, total = around(q2, x, x - 1, x + 1, r, lane)
            for i in range(CHUNKS):
                root = s[x * CHUNKS + i, pl.ds(r, 8), :]
                keep = a[x * CHUNKS + i, pl.ds(r, 8), :]
                full[x - HALO, pl.ds(r - 8, 8), pl.ds(LANES * i, LANES)] = (
                    keep * centre[i] / root + (conductance * root) * total[i]
                )
        return carry

    waited(low)
    outside(0, 0)

    def run(begin, end, *stages):
        def step(x, carry):
            for stage, shift in stages:
                stage(x + shift, 0)
            return carry

        lax.fori_loop(begin, end, step, 0)

    t, u, f, c = (third, -3), (second, -1), (first, 1), (inside, 0)
    stores = []
    waited(loads[0])
    run(0, 3, f, c)
    run(3, 4, u, f, c)
    waited(loads[1])
    run(4, 6, u, f, c)
    run(6, 8, t, u, f, c)
    waited(loads[2] + loads[3])
    run(8, 14, t, u, f, c)
    stores += started(pltpu.make_async_copy(full.at[pl.ds(0, 8)], out.at[pl.ds(0, 8)], sems.at[9]))
    run(14, 16, t, u, f, c)
    waited(high)
    outside(1, PLANES - HALO)
    run(16, 20, t, u, f)
    stores += started(pltpu.make_async_copy(full.at[pl.ds(8, 6)], out.at[pl.ds(8, 6)], sems.at[10]))
    run(20, 21, t, u)
    run(21, 22, t)
    stores += started(pltpu.make_async_copy(full.at[pl.ds(14, 2)], out.at[pl.ds(14, 2)], sems.at[11]))
    waited(ask)

    def answer(d, carry):
        value = jnp.zeros((8, LANES), F32)
        for c in range(3):
            cell = asked[d, c]
            x, y, z = cell >> 15, (cell >> 9) & 63, cell & 511
            lanes = pl.ds(pl.multiple_of((z >> 7) * LANES, LANES), LANES)
            tile = full[x, pl.ds(pl.multiple_of((y >> 3) * 8, 8), 8), lanes]
            tile = pltpu.roll(tile, (LANES + c - (z & 127)) & 127, 1)
            value = jnp.where(jnp.logical_and(row == (y & 7), lane == c), tile, value)
        answers[pl.ds(d, 1), :] = jnp.sum(value, axis=0, keepdims=True)
        return carry

    lax.fori_loop(0, NGX, answer, 0, unroll=4)
    waited(stores)


def diffusion(p, k, y_up, y_down, x_far, x_near, cells):
    return pl.pallas_call(
        diffusion_kernel,
        out_shape=(shape(CX, CY, NZ), shape(NGX, LANES)),
        in_specs=[spec(HBM)] * 2 + [spec()] * 2 + [spec(ANY)] * 3,
        out_specs=(spec(HBM), spec()),
        scratch_shapes=[VMEM((PLANES * CHUNKS, ROWS, LANES), F32) for _ in range(5)]
        + [VMEM((CX, CY, NZ), F32) for _ in range(3)]
        + [VMEM((2, 2 * HALO, CY + 8, NZ), F32), pltpu.SMEM((NGX, LANES), jnp.int32), DMA((14,))],
        compiler_params=pltpu.CompilerParams(vmem_limit_bytes=34 << 20),
        cost_estimate=pl.CostEstimate(flops=60_000_000, bytes_accessed=12_000_000, transcendentals=0),
        name="diffusion",
    )(far(p), far(k), y_up, y_down, x_far, x_near, cells)


def friction_kernel(rates, answers, terms, state_out, rate_out):
    known = terms[...]
    state, aged, normal, shear, direct, owners, rank = (known[i : i + 1, 0:TRI] for i in range(7))
    got = answers[...]
    named = lax.broadcasted_iota(jnp.int32, (NGX, TRI), 0).astype(F32) == owners
    held = jnp.zeros((NGX, TRI), F32)
    for c in range(3):
        held = jnp.where(jnp.logical_and(named, rank == float(c)), got[:, c : c + 1], held)
    pressure = jnp.sum(held, axis=0, keepdims=True)
    both = jnp.sum(rates[...], axis=0, keepdims=True)
    first, second = both[:, 0:TRI], both[:, TRI : 2 * TRI]
    effective = normal + step_time * second - pressure
    state_out[...] = state
    rate_out[...] = ((shear + step_time * first) / effective - friction_ref - aged) / direct


def friction(*values):
    return pl.pallas_call(
        friction_kernel,
        out_shape=(shape(1, TRI), shape(1, TRI)),
        in_specs=[spec()] * len(values),
        out_specs=(spec(), spec()),
        compiler_params=pltpu.CompilerParams(vmem_limit_bytes=4 << 20),
        name="friction",
    )(*values)


def exchanged(value, axis):
    return lax.all_to_all(value, axis, split_axis=0, concat_axis=0, tiled=True)


def local(
    pressure,
    permeability,
    kernel,
    slip_rate,
    aging_state,
    normal_stress,
    shear_stress,
    direct_effect,
    evolution_effect,
    slip_distance,
    tri_owner,
    tri_cell,
):
    rows = (
        tri_owner,
        tri_cell,
        slip_rate,
        aging_state,
        normal_stress,
        shear_stress,
        direct_effect,
        evolution_effect,
        slip_distance,
    )
    y_up, y_down, x_far, x_near = pack(pressure, permeability)
    wanted, terms = prepare(*[v.reshape(1, TRI) for v in rows])
    y_up, y_down = lax.ppermute(y_up, "gy", Y_UP), lax.ppermute(y_down, "gy", Y_DOWN)
    lane = lax.broadcasted_iota(jnp.int32, (NGX, LANES), 1)
    row = jnp.pad(lax.ppermute(slip_rate, ("gx", "gy"), SLIP_MOVES), (0, LANES - TRI)).reshape(1, LANES)
    leaving = jnp.where(lane < TRI, row, wanted)
    arrived = exchanged(leaving, "gx")
    x_far, x_near = sides(x_far, x_near, y_up, y_down, leaving)
    x_far, x_near = lax.ppermute(x_far, "gx", X_FAR), lax.ppermute(x_near, "gx", X_NEAR)
    partial_sums, cells = partial_rates(arrived, kernel)
    rates = exchanged(partial_sums, "gy")
    field, answers = diffusion(pressure, permeability, y_up, y_down, x_far, x_near, cells)
    answers = exchanged(answers, "gx")
    state_next, log_rate = friction(rates, answers, terms)
    return field, state_next.reshape(TRI), log_rate.reshape(TRI)


def solution(mesh):
    both = P(("gx", "gy"))
    placed = (
        P("gx", "gy", None),
        P("gx", "gy", None),
        P(None, "gx", "gy"),
        *([both] * 7),
        P(("gx", "gy"), None),
        both,
    )
    return jax.shard_map(
        local,
        mesh=mesh,
        in_specs=placed,
        out_specs=(P("gx", "gy", None), both, both),
        check_vma=False,
    )
```

```python
import jax
import jax.numpy as jnp
from jax import lax
from jax.experimental import pallas as pl
from jax.experimental.pallas import tpu as pltpu
from jax.sharding import PartitionSpec as P

NGX, NGY = 32, 8
CX, CY, NZ, TRI = 16, 64, 512, 48
HALO = 3
ROWS = 80
LANES = 128
CHUNKS = NZ // LANES
conductance = 0.15
step_time = 1.0
heal_time = 0.5
friction_ref = 0.6
F32 = jnp.float32
VMEM = pltpu.VMEM
ANY = pl.ANY

X_MOVE = (2, 1, 2, 1, 0, 3, 0, 3)
Y_MOVE = (1, 1, 0, 0, 0, 0, 1, 1)
X_CODE = sum(v << (2 * i) for i, v in enumerate(X_MOVE))
Y_CODE = sum(v << i for i, v in enumerate(Y_MOVE))


def landing(group, other):
    delta = (other - group) & 7
    x = ((group >> 1) + ((X_CODE >> (2 * delta)) & 3)) & 3
    y = (group & 1) ^ ((Y_CODE >> delta) & 1)
    return 2 * x + y


SLIP_MOVES = [
    ((4 * g + r) * NGY + j, (4 * landing(g, j) + r) * NGY + g) for g in range(8) for r in range(4) for j in range(NGY)
]
X_FAR = [pair for i in range(1, NGX - 1, 2) for pair in ((i, i + 1), (i + 1, i))]
X_NEAR = [pair for i in range(0, NGX, 2) for pair in ((i, i + 1), (i + 1, i))]
Y_FAR = [pair for i in range(1, NGY - 1, 2) for pair in ((i, i + 1), (i + 1, i))]
Y_NEAR = [pair for i in range(0, NGY, 2) for pair in ((i, i + 1), (i + 1, i))]


def spec(space=VMEM):
    return pl.BlockSpec(memory_space=space)


def shape(*dims, dtype=F32):
    return jax.ShapeDtypeStruct(dims, dtype)


def far(value):
    return pltpu.with_memory_space_constraint(value, pltpu.HBM)


def all_far(*values):
    return tuple(far(v) for v in values)


def core():
    return lax.rem(lax.axis_index("gx"), 2)


def sent_planes(core_index):
    return (CX - HALO) * core_index, (CX - HALO) * (1 - core_index)


def by_turn(first, second):
    odd = lax.rem(lax.axis_index("gy"), 2) == 1
    return jnp.where(odd, first, second), jnp.where(odd, second, first)


def started(*copies):
    for copy in copies:
        copy.start()
    return copies


def waited(copies):
    for copy in copies:
        copy.wait()


HBM = pltpu.HBM
DMA = pltpu.SemaphoreType.DMA


def turned(row_value):
    row = lax.broadcasted_iota(jnp.int32, (TRI, TRI), 0)
    column = lax.broadcasted_iota(jnp.int32, (TRI, TRI), 1)
    return jnp.sum(jnp.where(row == column, row_value, 0.0), axis=1, keepdims=True)


def pack_kernel(p, k, y_far, y_near, x_far, x_near, tiles, rows, sems):
    tops = started(
        pltpu.make_async_copy(p.at[:, pl.ds(CY - 8, 8), :], tiles.at[0], sems.at[0]),
        pltpu.make_async_copy(k.at[:, pl.ds(CY - 8, 8), :], tiles.at[1], sems.at[1]),
        pltpu.make_async_copy(p.at[:, pl.ds(0, 8), :], tiles.at[2], sems.at[2]),
        pltpu.make_async_copy(k.at[:, pl.ds(0, 8), :], tiles.at[3], sems.at[3]),
    )
    loads = [
        started(
            *[
                pltpu.make_async_copy(
                    source.at[pl.ds(start, HALO)], rows.at[side, pl.ds(HALO * n, HALO)], sems.at[4 + 2 * side + n]
                )
                for n, source in enumerate((p, k))
            ]
        )
        for side, start in enumerate(sent_planes(core()))
    ]
    row = lax.broadcasted_iota(jnp.int32, (8, NZ), 0)
    waited(tops)

    def plane(x, carry):
        top = jnp.where(row >= 5, tiles[0, x], pltpu.roll(tiles[1, x], 3, 0))
        bottom = jnp.where(row < 3, tiles[2, x], pltpu.roll(tiles[3, x], 5, 0))
        y_far[x], y_near[x] = by_turn(top, bottom)
        return carry

    lax.fori_loop(0, CX, plane, 0)
    stores = []
    for side, target in enumerate((x_far, x_near)):
        waited(loads[side])
        stores += started(pltpu.make_async_copy(rows.at[side], target.at[:, pl.ds(0, CY)], sems.at[8 + side]))
    waited(stores)


def pack(p, k):
    return pl.pallas_call(
        pack_kernel,
        out_shape=(shape(CX, 8, NZ),) * 2 + (HBM((2 * HALO, CY + 8, NZ), F32),) * 2,
        in_specs=[spec(HBM)] * 2,
        out_specs=(spec(),) * 2 + (spec(HBM),) * 2,
        scratch_shapes=[VMEM((4, CX, 8, NZ), F32), VMEM((2, 2 * HALO, CY, NZ), F32), DMA((10,))],
        compiler_params=pltpu.CompilerParams(vmem_limit_bytes=6 << 20),
        name="pack",
    )(far(p), far(k))


def prepare_kernel(owner, cell, *refs):
    floats, (wanted, terms, whole, held, sems) = refs[:7], refs[7:]
    waited(
        started(
            pltpu.make_async_copy(owner, whole.at[0], sems.at[0]),
            pltpu.make_async_copy(cell, whole.at[1], sems.at[1]),
            *[pltpu.make_async_copy(ref, held.at[n], sems.at[2 + n]) for n, ref in enumerate(floats)],
        )
    )
    slip, aging, normal, shear, direct, evolution, distance = (held[n] for n in range(7))
    owners = whole[0].astype(F32)
    first = lax.broadcasted_iota(jnp.int32, (TRI, TRI), 0)
    second = lax.broadcasted_iota(jnp.int32, (TRI, TRI), 1)
    same = jnp.logical_and(turned(owners) == owners, first < second)
    rank = jnp.sum(jnp.where(same, 1.0, 0.0), axis=0, keepdims=True)
    cells = whole[1].astype(F32)
    lane = lax.broadcasted_iota(jnp.int32, (NGX, LANES), 1)
    named = lax.broadcasted_iota(jnp.int32, (NGX, TRI), 0) == whole[0]
    value = jnp.zeros((NGX, LANES), F32)
    for c in range(3):
        asked = jnp.where(jnp.logical_and(named, rank == float(c)), cells, 0.0)
        value = jnp.where(lane == TRI + c, jnp.sum(asked, axis=1, keepdims=True), value)
    wanted[...] = value
    ratio = distance / slip
    state = ratio + (aging - ratio) * jnp.exp(-heal_time / ratio)
    terms[...] = jnp.zeros((8, LANES), F32)
    aged = evolution * jnp.log(state / distance)
    for n, term in enumerate((state, aged, normal, shear, direct, owners, rank)):
        terms[n : n + 1, 0:TRI] = term


def prepare(*values):
    return pl.pallas_call(
        prepare_kernel,
        out_shape=(shape(NGX, LANES), shape(8, LANES)),
        in_specs=[spec(HBM)] * len(values),
        out_specs=(spec(),) * 2,
        scratch_shapes=[VMEM((2, 1, TRI), jnp.int32), VMEM((7, 1, TRI), F32), DMA((9,))],
        compiler_params=pltpu.CompilerParams(vmem_limit_bytes=2 << 20),
        name="prepare",
    )(*all_far(*values))


def halo_rows(low, high, row):
    p = jnp.where(row >= 5, low, jnp.where(row < 3, high, 0.0))
    k = jnp.where(row >= 5, pltpu.roll(low, 5, 0), jnp.where(row < 3, pltpu.roll(high, 3, 0), 0.0))
    return p, k


def sides_kernel(x_far, x_near, y_far, y_near, token, x_far_out, x_near_out, tiles, sems):
    del x_far, x_near, token
    row = lax.broadcasted_iota(jnp.int32, (8, NZ), 0)
    copies = []
    for side, (target, start) in enumerate(zip((x_far_out, x_near_out), sent_planes(core()))):
        for n in range(HALO):
            tiles[side, n], tiles[side, HALO + n] = halo_rows(*by_turn(y_near[start + n], y_far[start + n]), row)
        copies += started(pltpu.make_async_copy(tiles.at[side], target.at[:, pl.ds(CY, 8)], sems.at[side]))
    waited(copies)


def sides(x_far, x_near, y_far, y_near, token):
    return pl.pallas_call(
        sides_kernel,
        out_shape=(HBM((2 * HALO, CY + 8, NZ), F32),) * 2,
        in_specs=[spec(HBM)] * 2 + [spec()] * 2 + [spec(ANY)],
        out_specs=(spec(HBM),) * 2,
        scratch_shapes=[VMEM((2, 2 * HALO, 8, NZ), F32), DMA((2,))],
        input_output_aliases={0: 0, 1: 1},
        compiler_params=pltpu.CompilerParams(vmem_limit_bytes=4 << 20),
        name="sides",
    )(far(x_far), far(x_near), y_far, y_near, token)


def rates_kernel(arrived, kernel_far, out, cells, acc, kernel, sems):
    copies = started(
        *[
            pltpu.make_async_copy(
                kernel_far.at[n // 4, pl.ds(96 * (n % 4), 96)], kernel.at[n // 4, pl.ds(96 * (n % 4), 96)], sems.at[n]
            )
            for n in range(8)
        ]
    )
    gy = lax.axis_index("gy")
    lane = lax.broadcasted_iota(jnp.int32, (1, LANES), 1)
    chunks = [jnp.zeros((1, LANES), F32) for _ in range(12)]
    for j in range(NGY):
        spot = landing(gy, j)
        for r in range(4):
            start = (r * NGY + j) * TRI
            chunk, offset = divmod(start, LANES)
            row = pltpu.roll(arrived[pl.ds(4 * spot + r, 1), :], offset, 1)
            inside = jnp.logical_and(lane >= offset, lane < offset + TRI)
            chunks[chunk] = jnp.where(inside, row, chunks[chunk])
            if offset + TRI > LANES:
                chunks[chunk + 1] = jnp.where(lane < offset + TRI - LANES, row, chunks[chunk + 1])
    cells[...] = pltpu.roll(arrived[...], LANES - TRI, 1).astype(jnp.int32)
    wide = [jnp.broadcast_to(c, (8, LANES)) for c in chunks]

    for n in range(8):
        part = n // 4
        copies[n].wait()

        def tile(t, carry):
            rows = pl.ds(pl.multiple_of(t * 8, 8), 8)
            terms = [kernel[part, rows, pl.ds(LANES * c, LANES)] * wide[c] for c in range(12)]
            while len(terms) > 1:
                terms = [a + b for a, b in zip(terms[::2], terms[1::2])] + terms[len(terms) // 2 * 2 :]
            dest = (t // 6) * 96 + part * TRI + (t % 6) * 8
            acc[pl.ds(pl.multiple_of(dest, 8), 8), :] = terms[0]
            return carry

        lax.fori_loop(12 * (n % 4), 12 * (n % 4) + 12, tile, 0, unroll=4)
    row8 = lax.broadcasted_iota(jnp.int32, (8, LANES), 0)
    total = jnp.zeros((8, 2 * TRI), F32)
    for j in range(NGY):
        total = total + lax.dot_general(
            jnp.where(row8 == j, 1.0, 0.0),
            acc[pl.ds(2 * TRI * j, 2 * TRI), :],
            (((1,), (1,)), ((), ())),
            precision=lax.Precision.HIGHEST,
            preferred_element_type=F32,
        )
    out[...] = jnp.zeros((8, LANES), F32)
    out[:, 0 : 2 * TRI] = total


def partial_rates(arrived, kernel):
    return pl.pallas_call(
        rates_kernel,
        out_shape=(shape(NGY, LANES), shape(NGX, LANES, dtype=jnp.int32)),
        in_specs=[spec(), spec(HBM)],
        out_specs=(spec(), spec()),
        scratch_shapes=[VMEM((768, LANES), F32), VMEM(kernel.shape, F32), DMA((8,))],
        compiler_params=pltpu.CompilerParams(vmem_limit_bytes=8 << 20),
        cost_estimate=pl.CostEstimate(flops=1000000000000, bytes_accessed=6000000000, transcendentals=0),
        name="rates",
    )(arrived, far(kernel))


def around(ref, x, before, after, row, lane):
    rows = pl.ds(row, 8)
    centre = [ref[x * CHUNKS + i, rows, :] for i in range(CHUNKS)]
    left = [pltpu.roll(v, 1, 1) for v in centre]
    right = [pltpu.roll(v, LANES - 1, 1) for v in centre]
    sums = []
    for i in range(CHUNKS):
        below = left[i - 1] if i else 0.0
        above = right[i + 1] if i + 1 < CHUNKS else 0.0
        z = jnp.where(lane == 0, below, left[i]) + jnp.where(lane == LANES - 1, above, right[i])
        y = ref[x * CHUNKS + i, pl.ds(row - 1, 8), :] + ref[x * CHUNKS + i, pl.ds(row + 1, 8), :]
        xs = ref[before * CHUNKS + i, rows, :] + ref[after * CHUNKS + i, rows, :]
        sums.append((xs + y) + z)
    return centre, sums


PLANES = CX + 2 * HALO


def diffusion_kernel(
    p_far, k_far, y_far, y_near, x_far, x_near, cells, out, answers, s, q, a, q1, q2, p, k, full, wide, asked, sems
):
    loads = []
    odd = core()
    started(pltpu.make_async_copy(x_far, wide.at[odd], sems.at[12 + odd]))
    started(pltpu.make_async_copy(x_near, wide.at[1 - odd], sems.at[13 - odd]))
    for n in range(4):
        planes = pl.ds(4 * n, 4)
        loads.append(
            started(
                pltpu.make_async_copy(p_far.at[planes], p.at[planes], sems.at[2 * n]),
                pltpu.make_async_copy(k_far.at[planes], k.at[planes], sems.at[2 * n + 1]),
            )
        )
    low = [pltpu.make_async_copy(x_far, wide.at[0], sems.at[12])]
    high = [pltpu.make_async_copy(x_near, wide.at[1], sems.at[13])]
    ask = started(pltpu.make_async_copy(cells, asked, sems.at[8]))
    lane = lax.broadcasted_iota(jnp.int32, (8, LANES), 1)
    row = lax.broadcasted_iota(jnp.int32, (8, LANES), 0)

    def put(n, places, p_tile, k_tile):
        root = jnp.sqrt(k_tile)
        scaled = root * p_tile
        for place in places:
            s[n, place : place + 8, :] = root
            q[n, place : place + 8, :] = scaled

    def outside(side, base):
        def plane(n, carry):
            for i in range(CHUNKS):
                lanes = pl.ds(LANES * i, LANES)
                for t in range(CY // 8 + 1):
                    places = (8 * t + 8,) if t < CY // 8 else (0, CY + 8)
                    rows = pl.ds(8 * t, 8)
                    put((base + n) * CHUNKS + i, places, wide[side, n, rows, lanes], wide[side, HALO + n, rows, lanes])
            return carry

        lax.fori_loop(0, HALO, plane, 0)

    def inside(x, carry):
        for i in range(CHUNKS):
            lanes = pl.ds(LANES * i, LANES)
            n = (x + HALO) * CHUNKS + i
            put(n, (0, CY + 8), *halo_rows(*by_turn(y_near[x, :, lanes], y_far[x, :, lanes]), row))
            for t in range(CY // 8):
                rows = pl.ds(8 * t, 8)
                put(n, (8 * t + 8,), p[x, rows, lanes], k[x, rows, lanes])
        return carry

    def first(x, carry):
        for r in range(6, 74, 8):
            root, sums = around(s, x, x - 1, x + 1, r, lane)
            centre, total = around(q, x, x - 1, x + 1, r, lane)
            for i in range(CHUNKS):
                scaled = conductance * root[i]
                keep = 1.0 - scaled * sums[i]
                a[x * CHUNKS + i, pl.ds(r, 8), :] = keep
                q1[x * CHUNKS + i, pl.ds(r, 8), :] = keep * centre[i] + (scaled * root[i]) * total[i]
        return carry

    def second(x, carry):
        for r in range(7, 73, 8):
            centre, total = around(q1, x, x - 1, x + 1, r, lane)
            for i in range(CHUNKS):
                root = s[x * CHUNKS + i, pl.ds(r, 8), :]
                keep = a[x * CHUNKS + i, pl.ds(r, 8), :]
                q2[x * CHUNKS + i, pl.ds(r, 8), :] = keep * centre[i] + (conductance * root * root) * total[i]
        return carry

    def third(x, carry):
        for r in range(8, 72, 8):
            centre, total = around(q2, x, x - 1, x + 1, r, lane)
            for i in range(CHUNKS):
                root = s[x * CHUNKS + i, pl.ds(r, 8), :]
                keep = a[x * CHUNKS + i, pl.ds(r, 8), :]
                full[x - HALO, pl.ds(r - 8, 8), pl.ds(LANES * i, LANES)] = (
                    keep * centre[i] / root + (conductance * root) * total[i]
                )
        return carry

    waited(low)
    outside(0, 0)

    def run(begin, end, *stages):
        def step(x, carry):
            for stage, shift in stages:
                stage(x + shift, 0)
            return carry

        lax.fori_loop(begin, end, step, 0)

    t, u, f, c = (third, -3), (second, -1), (first, 1), (inside, 0)
    stores = []
    waited(loads[0])
    run(0, 3, f, c)
    run(3, 4, u, f, c)
    waited(loads[1])
    run(4, 6, u, f, c)
    run(6, 8, t, u, f, c)
    waited(loads[2] + loads[3])
    run(8, 14, t, u, f, c)
    stores += started(pltpu.make_async_copy(full.at[pl.ds(0, 8)], out.at[pl.ds(0, 8)], sems.at[9]))
    run(14, 16, t, u, f, c)
    waited(high)
    outside(1, PLANES - HALO)
    run(16, 20, t, u, f)
    stores += started(pltpu.make_async_copy(full.at[pl.ds(8, 6)], out.at[pl.ds(8, 6)], sems.at[10]))
    run(20, 21, t, u)
    run(21, 22, t)
    stores += started(pltpu.make_async_copy(full.at[pl.ds(14, 2)], out.at[pl.ds(14, 2)], sems.at[11]))
    waited(ask)

    def answer(d, carry):
        value = jnp.zeros((8, LANES), F32)
        for c in range(3):
            cell = asked[d, c]
            x, y, z = cell >> 15, (cell >> 9) & 63, cell & 511
            lanes = pl.ds(pl.multiple_of((z >> 7) * LANES, LANES), LANES)
            tile = full[x, pl.ds(pl.multiple_of((y >> 3) * 8, 8), 8), lanes]
            tile = pltpu.roll(tile, (LANES + c - (z & 127)) & 127, 1)
            value = jnp.where(jnp.logical_and(row == (y & 7), lane == c), tile, value)
        answers[pl.ds(d, 1), :] = jnp.sum(value, axis=0, keepdims=True)
        return carry

    lax.fori_loop(0, NGX, answer, 0, unroll=4)
    waited(stores)


def diffusion(p, k, y_far, y_near, x_far, x_near, cells):
    return pl.pallas_call(
        diffusion_kernel,
        out_shape=(shape(CX, CY, NZ), shape(NGX, LANES)),
        in_specs=[spec(HBM)] * 2 + [spec()] * 2 + [spec(ANY)] * 3,
        out_specs=(spec(HBM), spec()),
        scratch_shapes=[VMEM((PLANES * CHUNKS, ROWS, LANES), F32) for _ in range(5)]
        + [VMEM((CX, CY, NZ), F32) for _ in range(3)]
        + [VMEM((2, 2 * HALO, CY + 8, NZ), F32), pltpu.SMEM((NGX, LANES), jnp.int32), DMA((14,))],
        compiler_params=pltpu.CompilerParams(vmem_limit_bytes=34 << 20),
        cost_estimate=pl.CostEstimate(flops=60_000_000, bytes_accessed=12_000_000, transcendentals=0),
        name="diffusion",
    )(far(p), far(k), y_far, y_near, x_far, x_near, cells)


def friction_kernel(rates, answers, terms, state_out, rate_out):
    known = terms[...]
    state, aged, normal, shear, direct, owners, rank = (known[i : i + 1, 0:TRI] for i in range(7))
    got = answers[...]
    named = lax.broadcasted_iota(jnp.int32, (NGX, TRI), 0).astype(F32) == owners
    held = jnp.zeros((NGX, TRI), F32)
    for c in range(3):
        held = jnp.where(jnp.logical_and(named, rank == float(c)), got[:, c : c + 1], held)
    pressure = jnp.sum(held, axis=0, keepdims=True)
    both = jnp.sum(rates[...], axis=0, keepdims=True)
    first, second = both[:, 0:TRI], both[:, TRI : 2 * TRI]
    effective = normal + step_time * second - pressure
    state_out[...] = state
    rate_out[...] = ((shear + step_time * first) / effective - friction_ref - aged) / direct


def friction(*values):
    return pl.pallas_call(
        friction_kernel,
        out_shape=(shape(1, TRI), shape(1, TRI)),
        in_specs=[spec()] * len(values),
        out_specs=(spec(), spec()),
        compiler_params=pltpu.CompilerParams(vmem_limit_bytes=4 << 20),
        name="friction",
    )(*values)


def exchanged(value, axis):
    return lax.all_to_all(value, axis, split_axis=0, concat_axis=0, tiled=True)


def local(
    pressure,
    permeability,
    kernel,
    slip_rate,
    aging_state,
    normal_stress,
    shear_stress,
    direct_effect,
    evolution_effect,
    slip_distance,
    tri_owner,
    tri_cell,
):
    rows = (
        tri_owner,
        tri_cell,
        slip_rate,
        aging_state,
        normal_stress,
        shear_stress,
        direct_effect,
        evolution_effect,
        slip_distance,
    )
    y_far, y_near, x_far, x_near = pack(pressure, permeability)
    wanted, terms = prepare(*[v.reshape(1, TRI) for v in rows])
    y_far, y_near = lax.ppermute(y_far, "gy", Y_FAR), lax.ppermute(y_near, "gy", Y_NEAR)
    lane = lax.broadcasted_iota(jnp.int32, (NGX, LANES), 1)
    row = jnp.pad(lax.ppermute(slip_rate, ("gx", "gy"), SLIP_MOVES), (0, LANES - TRI)).reshape(1, LANES)
    leaving = jnp.where(lane < TRI, row, wanted)
    arrived = exchanged(leaving, "gx")
    x_far, x_near = sides(x_far, x_near, y_far, y_near, leaving)
    x_far, x_near = lax.ppermute(x_far, "gx", X_FAR), lax.ppermute(x_near, "gx", X_NEAR)
    partial_sums, cells = partial_rates(arrived, kernel)
    rates = exchanged(partial_sums, "gy")
    field, answers = diffusion(pressure, permeability, y_far, y_near, x_far, x_near, cells)
    answers = exchanged(answers, "gx")
    state_next, log_rate = friction(rates, answers, terms)
    return field, state_next.reshape(TRI), log_rate.reshape(TRI)


def solution(mesh):
    both = P(("gx", "gy"))
    placed = (
        P("gx", "gy", None),
        P("gx", "gy", None),
        P(None, "gx", "gy"),
        *([both] * 7),
        P(("gx", "gy"), None),
        both,
    )
    return jax.shard_map(
        local,
        mesh=mesh,
        in_specs=placed,
        out_specs=(P("gx", "gy", None), both, both),
        check_vma=False,
    )
```
